32 devices in a mesh: cd: 8 (over z, y), ab: 4 (over x, core).
Axes of the slice: x: 2, y: 2, z: 4, core: 2. Of those that a mesh axis runs over, the one named last changes fastest.
Arguments:
- amplitudes: float32 [2, 128, 57344], P(None, 'ab', 'cd'), may hold values from -6 to 6
- integrals: float32 [57344, 1536], P('cd', 'ab'), may hold values from -0.0234375 to 0.0234375
- c_index: int32 [57344], P('cd'), may hold values from 0 to 1532, as said below
- d_index: int32 [57344], P('cd'), may hold values from 0 to 1535
- a_index: int32 [1536], P('ab'), may hold values from 0 to 1532, as said below
- b_index: int32 [1536], P('ab'), may hold values from 0 to 1535
Outputs:
- ladder: float32 [128, 2, 1536], P('cd', None, 'ab')
The draws below stay inside these ranges and needn't reach their ends.
Inputs may be any that keep to these rules, and one draw needn't show every extreme that they name: c_index[p] <= d_index[p] for every pair; some pairs have c_index equal to d_index. a_index[q] <= b_index[q] for every result pair; some have a_index equal to b_index.
All inputs are finite; a program needn't handle non-finite values.
Results may differ from the reference program's by a relative error of at most 0.00007.
Values sent between devices are 32-bit elements; how exact they have to be, the bound alone decides.
A program may use at most 64 MiB of HBM per device.

```python
import jax
import jax.numpy as jnp
from jax import lax

NV = 1536
IJ = 128
PAIRS = 57344
COLS = 1536


def pair_draw(key, count, salt):
    key = jax.random.fold_in(key, salt)
    first_key, off_key = jax.random.split(key)
    first = jax.random.randint(first_key, (count,), 0, NV - 3, dtype=jnp.int32)
    offset = jax.random.randint(off_key, (count,), 0, 4, dtype=jnp.int32)
    first = first.at[0].set(0).at[count - 1].set(NV - 4)
    offset = offset.at[0].set(0).at[count - 1].set(3)
    return (first, first + offset)


def draw_c_index(key, part):
    first, second = pair_draw(key, PAIRS, 11)
    return first


def draw_d_index(key, part):
    first, second = pair_draw(key, PAIRS, 11)
    return second


def draw_a_index(key, part):
    first, second = pair_draw(key, COLS, 23)
    return first


def draw_b_index(key, part):
    first, second = pair_draw(key, COLS, 23)
    return second


def with_spikes(result, rng, source, target, blocks, factor):
    owner, partner = [(jnp.arange(result.shape[position]) // (result.shape[position] // blocks)).reshape([-1 if axis == position else 1 for axis in range(result.ndim)]) for position in (source, target)]
    chosen = jax.random.permutation(rng, blocks)[partner]
    strong = (owner == chosen) | (owner == (partner + blocks // 2) % blocks)
    return jnp.where(strong, factor * result, result)


def levels(own_key, extent, cuts, smallest, top_value):
    level, own = 1.0, jax.random.fold_in(own_key, 6)
    for axis_at, blocks in cuts:
        draws = jnp.exp(jax.random.uniform(jax.random.fold_in(own, axis_at), (blocks,), jnp.float32, smallest / len(cuts), top_value / len(cuts)))
        level = level * jnp.repeat(draws, extent[axis_at] // blocks).reshape([-1 if axis == axis_at else 1 for axis in range(len(extent))])
    return level


def gaussian(stream_key, extent, scale, reach, cuts=(), held_as=jnp.bfloat16):
    drawn = jax.random.normal(stream_key, extent, jnp.float32) * scale
    if len(cuts) > 0:
        drawn = levels(stream_key, extent, cuts, -0.22, 0.18) * drawn
    return jnp.clip(drawn, min=-reach, max=reach).astype(held_as)


def heavy_noise(stream_key, shape, width, most, shards, heavy, held_as=jnp.bfloat16):
    array = width * jax.random.normal(stream_key, shape, jnp.float32)
    if shards:
        array = array * levels(stream_key, shape, shards, -0.22, 0.18)
    return jnp.clip(with_spikes(array, jax.random.fold_in(stream_key, 3), *heavy), -most, most).astype(held_as)


def setup_inputs(seed: int = 0) -> dict:
    seeds = jax.random.split(jax.random.key(seed), 7)
    amplitudes = heavy_noise(seeds[0], (2, IJ, PAIRS), 1.0, 6.0, ((1, 4), (2, 8)), (2, 1, 8, 2.0), jnp.float32)
    integrals = gaussian(seeds[1], (PAIRS, COLS), PAIRS ** -0.5, 0.0234375, ((0, 8), (1, 4)), jnp.float32)
    c_index = draw_c_index(jax.random.fold_in(seeds[6], 71), 0)
    d_index = draw_d_index(jax.random.fold_in(seeds[6], 71), 0)
    a_index = draw_a_index(jax.random.fold_in(seeds[6], 71), 0)
    b_index = draw_b_index(jax.random.fold_in(seeds[6], 71), 0)
    return dict(amplitudes=amplitudes, integrals=integrals, c_index=c_index, d_index=d_index, a_index=a_index, b_index=b_index)


def reference(amplitudes, integrals, c_index, d_index, a_index, b_index):
    same = c_index == d_index
    weight_plus = jnp.where(same, jnp.float32(0.5), jnp.float32(1.0))
    weight_minus = jnp.where(same, jnp.float32(0.0), jnp.float32(1.0))
    weights = jnp.stack([weight_plus, weight_minus])
    weighted = amplitudes * weights[:, None, :]
    summed = jnp.einsum("sip,pq->isq", weighted, integrals, precision=lax.Precision.HIGHEST)
    keep = jnp.where(a_index == b_index, jnp.float32(0.0), jnp.float32(1.0))
    factor = 0.5 * jnp.stack([jnp.ones_like(keep), keep])
    return summed * factor[None, :, :]
```

```python
import functools

import jax
import jax.numpy as jnp
from jax import lax
from jax.experimental import pallas as pl
from jax.experimental.pallas import tpu as pltpu
from jax.sharding import PartitionSpec as P

MESH = pl.DeviceIdType.MESH
BF16 = jnp.bfloat16
F32 = jnp.float32

ROWS = 16
DEPTH = 1024
AHEAD = 4


def split(x):
    high = x.astype(BF16)
    return high, (x - high.astype(F32)).astype(BF16)


def kernel(n, a_hbm, v_hbm, c_ref, d_ref, qa_ref, qb_ref, out_ref,
           held, v, v_high, v_low, weights, total, near, part, recv,
           own_sem, v_sem, cs, cr, xs, xr, fs, fr, rs, rr):
    me = lax.axis_index("cd")
    j = lax.axis_index("ab")
    beside = j + 1 - 2 * lax.rem(j, 2)
    across = lax.rem(j + 2, 4)
    far = lax.rem(beside + 2, 4)
    block = a_hbm.shape[1]
    depth = a_hbm.shape[2]
    pieces = depth // DEPTH
    steps = block // ROWS * pieces
    unit = part.shape[2]
    mine = recv.shape[1]

    own = pltpu.make_async_copy(a_hbm, held.at[0], own_sem)
    own.start()

    def v_copy(k):
        at = pl.ds(pl.multiple_of(k * DEPTH, DEPTH), DEPTH)
        return pltpu.make_async_copy(v_hbm.at[at], v.at[at], v_sem.at[k])

    @pl.loop(0, pieces)
    def _(k):
        v_copy(k).start()

    barrier = pltpu.get_barrier_semaphore()
    for other in (beside, across):
        pl.semaphore_signal(barrier, inc=1, device_id={"ab": other}, device_id_type=MESH)

    @pl.loop(1, n)
    def _(step):
        pl.semaphore_signal(
            barrier, inc=1, device_id={"cd": lax.rem(me + step, n)}, device_id_type=MESH
        )

    pl.semaphore_wait(barrier, n + 1)

    def columns(k):
        return pl.ds(pl.multiple_of(k * DEPTH, DEPTH), DEPTH)

    def window(t):
        rows = pl.ds(pl.multiple_of(t // pieces * ROWS, ROWS), ROWS)
        return rows, columns(lax.rem(t, pieces))

    def cross_copy(t):
        rows, cols = window(t)
        return pltpu.make_async_remote_copy(
            src_ref=a_hbm.at[:, rows, cols], dst_ref=held.at[2, :, rows, cols],
            send_sem=xs.at[t], recv_sem=xr.at[t],
            device_id={"ab": across}, device_id_type=MESH,
        )

    def pass_copy(t):
        rows, cols = window(t)
        return pltpu.make_async_remote_copy(
            src_ref=held.at[2, :, rows, cols], dst_ref=held.at[3, :, rows, cols],
            send_sem=fs.at[t], recv_sem=fr.at[t],
            device_id={"ab": beside}, device_id_type=MESH,
        )

    def near_copy(k):
        cols = columns(k)
        return pltpu.make_async_remote_copy(
            src_ref=a_hbm.at[:, :, cols], dst_ref=held.at[1, :, :, cols],
            send_sem=cs.at[k], recv_sem=cr.at[k],
            device_id={"ab": beside}, device_id_type=MESH,
        )

    @pl.loop(0, min(AHEAD, steps))
    def _(t):
        cross_copy(t).start()

    @pl.loop(0, pieces)
    def _(k):
        near_copy(k).start()

    same = c_ref[...] == d_ref[...]
    weights[0:1, :] = jnp.where(same, F32(0.5), F32(1.0))
    weights[1:2, :] = jnp.where(same, F32(0.0), F32(1.0))

    def product(first, second, rows, cols):
        plus, minus = weights[0:1, cols], weights[1:2, cols]
        x = jnp.concatenate([
            held[first, 0, rows, cols] * plus, held[first, 1, rows, cols] * minus,
            held[second, 0, rows, cols] * plus, held[second, 1, rows, cols] * minus,
        ], axis=0)
        high, low = split(x)
        count = x.shape[0]
        by_high = jnp.dot(jnp.concatenate([high, low], axis=0), v_high[cols, :],
                          preferred_element_type=F32)
        by_low = jnp.dot(high, v_low[cols, :], preferred_element_type=F32)
        return by_high[:count] + by_high[count:] + by_low

    def send_sums(row, sums):
        for m in range(8 // unit):
            message = row // unit + m
            for s in range(2):
                part[message, s] = sums[s][m * unit:(m + 1) * unit]
            owner = message // mine

            @pl.when(owner != me)
            def _():
                pltpu.make_async_remote_copy(
                    src_ref=part.at[message],
                    dst_ref=recv.at[lax.rem(me - owner - 1 + n, n), lax.rem(message, mine)],
                    send_sem=rs, recv_sem=rr,
                    device_id={"cd": owner}, device_id_type=MESH,
                ).start()

    own.wait()
    near[...] = jnp.zeros_like(near)

    @pl.loop(0, pieces)
    def _(k):
        cols = columns(k)
        v_copy(k).wait()
        v_high[cols, :], v_low[cols, :] = split(v[cols, :])
        near_copy(k).wait_recv()
        near[...] += product(0, 1, pl.ds(0, block), cols)

    for at, owner in ((0, j), (1, beside)):
        for row in range(0, block, 8):
            base = at * 2 * block + row
            send_sums(owner * block + row,
                      [near[base + s * block:base + s * block + 8, :] for s in range(2)])

    @pl.loop(0, steps)
    def _(t):
        rows, cols = window(t)
        cross_copy(t).wait_recv()
        pass_copy(t).start()
        cross_copy(t).wait_send()

        @pl.when(t + AHEAD < steps)
        def _():
            cross_copy(t + AHEAD).start()

        @pl.when(lax.rem(t, pieces) == 0)
        def _():
            total[...] = jnp.zeros_like(total)

        pass_copy(t).wait_recv()
        total[...] += product(2, 3, rows, cols)

        @pl.when(lax.rem(t, pieces) == pieces - 1)
        def _():
            for at, owner in ((0, across), (1, far)):
                for row in range(0, ROWS, 8):
                    base = at * 2 * ROWS + row
                    send_sums(owner * block + t // pieces * ROWS + row,
                              [total[base + s * ROWS:base + s * ROWS + 8, :] for s in range(2)])

    keep = jnp.where(qa_ref[...] == qb_ref[...], F32(0.0), F32(0.5))
    pltpu.make_async_copy(recv, recv, rr).wait()
    for m in range(mine):
        sums = part[me * mine + m]
        sums = lax.fori_loop(0, n - 1, lambda k, acc: acc + recv[k, m], sums)
        out_ref[0, m * unit:(m + 1) * unit, :] = sums[0] * F32(0.5)
        out_ref[1, m * unit:(m + 1) * unit, :] = sums[1] * keep

    pltpu.make_async_copy(recv, recv, rs).wait()

    @pl.loop(0, pieces)
    def _(k):
        near_copy(k).wait_send()

    @pl.loop(0, steps)
    def _(t):
        pass_copy(t).wait_send()


def local(n, amplitudes, integrals, c_index, d_index, a_index, b_index):
    _, block, depth = amplitudes.shape
    q = integrals.shape[1]
    rows = 4 * block // n
    unit = min(8, rows)
    pieces = depth // DEPTH
    steps = block // ROWS * pieces
    dma = pltpu.SemaphoreType.DMA
    whole = pl.BlockSpec(memory_space=pltpu.VMEM)
    out = pl.pallas_call(
        functools.partial(kernel, n),
        out_shape=jax.ShapeDtypeStruct((2, rows, q), F32),
        in_specs=[pl.BlockSpec(memory_space=pl.ANY)] * 2 + [whole] * 4,
        out_specs=whole,
        scratch_shapes=[
            pltpu.VMEM((4, 2, block, depth), F32),
            pltpu.VMEM((depth, q), F32),
            pltpu.VMEM((depth, q), BF16),
            pltpu.VMEM((depth, q), BF16),
            pltpu.VMEM((2, depth), F32),
            pltpu.VMEM((4 * ROWS, q), F32),
            pltpu.VMEM((4 * block, q), F32),
            pltpu.VMEM((4 * block // unit, 2, unit, q), F32),
            pltpu.VMEM((n - 1, rows // unit, 2, unit, q), F32),
            dma, dma((pieces,)), dma((pieces,)), dma((pieces,)),
            dma((steps,)), dma((steps,)), dma((steps,)), dma((steps,)), dma, dma,
        ],
        compiler_params=pltpu.CompilerParams(
            collective_id=0, has_side_effects=True, vmem_limit_bytes=56 * 1024 * 1024
        ),
        cost_estimate=pl.CostEstimate(
            flops=3 * 2 * 8 * block * depth * q,
            bytes_accessed=4 * depth * (q + 2 * block), transcendentals=0,
        ),
    )(amplitudes, integrals, c_index.reshape(1, -1), d_index.reshape(1, -1),
      a_index.reshape(1, -1), b_index.reshape(1, -1))
    return jnp.transpose(out, (1, 0, 2))


def solution(mesh):
    placed = (P(None, "ab", "cd"), P("cd", "ab"), P("cd"), P("cd"), P("ab"), P("ab"))
    return jax.shard_map(
        functools.partial(local, mesh.shape["cd"]), mesh=mesh, in_specs=placed,
        out_specs=P("cd", None, "ab"), check_vma=False,
    )
```

```python
import functools

import jax
import jax.numpy as jnp
from jax import lax
from jax.experimental import pallas as pl
from jax.experimental.pallas import tpu as pltpu
from jax.sharding import PartitionSpec as P

MESH = pl.DeviceIdType.MESH
BF16 = jnp.bfloat16
F32 = jnp.float32

LAST = 8
DEPTH = 1024


def split(x):
    high = x.astype(BF16)
    return high, (x - high.astype(F32)).astype(BF16)


def kernel(n, a_hbm, v_hbm, c_ref, d_ref, qa_ref, qb_ref, out_ref,
           held, v, v_split, weights, total, near, part, recv,
           own_sem, v_sem, cs, cr, xs, xr, fs, fr, rs, rr):
    me = lax.axis_index("cd")
    j = lax.axis_index("ab")
    beside = j + 1 - 2 * lax.rem(j, 2)
    across = lax.rem(j + 2, 4)
    far = lax.rem(beside + 2, 4)
    block = a_hbm.shape[1]
    depth = a_hbm.shape[2]
    pieces = depth // DEPTH
    q = out_ref.shape[2]
    chunks = ((0, block - LAST), (block - LAST, LAST))
    unit = part.shape[2]
    mine = recv.shape[1]

    own = pltpu.make_async_copy(a_hbm, held.at[0], own_sem)
    own.start()

    def v_copy(k):
        at = pl.ds(pl.multiple_of(k * DEPTH, DEPTH), DEPTH)
        return pltpu.make_async_copy(v_hbm.at[at], v.at[at], v_sem.at[k])

    @pl.loop(0, pieces)
    def _(k):
        v_copy(k).start()

    barrier = pltpu.get_barrier_semaphore()
    for other in (beside, across):
        pl.semaphore_signal(barrier, inc=1, device_id={"ab": other}, device_id_type=MESH)

    @pl.loop(1, n)
    def _(step):
        pl.semaphore_signal(
            barrier, inc=1, device_id={"cd": lax.rem(me + step, n)}, device_id_type=MESH
        )

    pl.semaphore_wait(barrier, n + 1)

    def columns(k):
        return pl.ds(pl.multiple_of(k * DEPTH, DEPTH), DEPTH)

    def window(chunk, k):
        return pl.ds(*chunks[chunk]), columns(k)

    def cross_copy(chunk, k):
        rows, cols = window(chunk, k)
        return pltpu.make_async_remote_copy(
            src_ref=a_hbm.at[:, rows, cols], dst_ref=held.at[2, :, rows, cols],
            send_sem=xs.at[chunk, k], recv_sem=xr.at[chunk, k],
            device_id={"ab": across}, device_id_type=MESH,
        )

    def pass_copy(chunk, k):
        rows, cols = window(chunk, k)
        return pltpu.make_async_remote_copy(
            src_ref=held.at[2, :, rows, cols], dst_ref=held.at[3, :, rows, cols],
            send_sem=fs.at[chunk, k], recv_sem=fr.at[chunk, k],
            device_id={"ab": beside}, device_id_type=MESH,
        )

    def near_copy(k):
        cols = columns(k)
        return pltpu.make_async_remote_copy(
            src_ref=a_hbm.at[:, :, cols], dst_ref=held.at[1, :, :, cols],
            send_sem=cs.at[k], recv_sem=cr.at[k],
            device_id={"ab": beside}, device_id_type=MESH,
        )

    @pl.loop(0, pieces)
    def _(k):
        cross_copy(0, k).start()

    @pl.loop(0, pieces)
    def _(k):
        near_copy(k).start()

    same = c_ref[...] == d_ref[...]
    weights[0:1, :] = jnp.where(same, F32(0.5), F32(1.0))
    weights[1:2, :] = jnp.where(same, F32(0.0), F32(1.0))

    def product(first, second, rows, cols):
        plus, minus = weights[0:1, cols], weights[1:2, cols]
        x = jnp.concatenate([
            held[first, 0, rows, cols] * plus, held[first, 1, rows, cols] * minus,
            held[second, 0, rows, cols] * plus, held[second, 1, rows, cols] * minus,
        ], axis=0)
        high, low = split(x)
        count = x.shape[0]
        out = jnp.dot(jnp.concatenate([high, low], axis=0), v_split[cols, :],
                      preferred_element_type=F32)
        return out[:count, :q] + (out[count:, :q] + out[:count, q:])

    def send_sums(row, sums):
        for m in range(8 // unit):
            message = row // unit + m
            for s in range(2):
                part[message, s] = sums[s][m * unit:(m + 1) * unit]
            owner = message // mine

            @pl.when(owner != me)
            def _():
                pltpu.make_async_remote_copy(
                    src_ref=part.at[message],
                    dst_ref=recv.at[lax.rem(me - owner - 1 + n, n), lax.rem(message, mine)],
                    send_sem=rs, recv_sem=rr,
                    device_id={"cd": owner}, device_id_type=MESH,
                ).start()

    own.wait()
    near[...] = jnp.zeros_like(near)

    @pl.loop(0, pieces)
    def _(k):
        cols = columns(k)
        v_copy(k).wait()
        v_split[cols, :q], v_split[cols, q:] = split(v[cols, :])
        near_copy(k).wait_recv()
        near[...] += product(0, 1, pl.ds(0, block), cols)

    for at, owner in ((0, j), (1, beside)):
        for row in range(0, block, 8):
            base = at * 2 * block + row
            send_sums(owner * block + row,
                      [near[base + s * block:base + s * block + 8, :] for s in range(2)])

    for chunk, (start, count) in enumerate(chunks):
        size = 4 * count
        total[:size, :] = jnp.zeros((size, q), F32)

        def add(k):
            rows, cols = window(chunk, k)
            pass_copy(chunk, k).wait_recv()
            total[:size, :] += product(2, 3, rows, cols)

        @pl.loop(0, pieces)
        def _(k):
            cross_copy(chunk, k).wait_recv()
            pass_copy(chunk, k).start()
            cross_copy(chunk, k).wait_send()
            if chunk == 0:
                cross_copy(1, k).start()

            @pl.when(k > 0)
            def _():
                add(k - 1)

        add(pieces - 1)
        for at, owner in ((0, across), (1, far)):
            for row in range(0, count, 8):
                base = at * 2 * count + row
                send_sums(owner * block + start + row,
                          [total[base + s * count:base + s * count + 8, :] for s in range(2)])

    keep = jnp.where(qa_ref[...] == qb_ref[...], F32(0.0), F32(0.5)).reshape(1, q)
    pltpu.make_async_copy(recv, recv, rr).wait()
    for m in range(mine):
        sums = part[me * mine + m]
        sums = lax.fori_loop(0, n - 1, lambda k, acc: acc + recv[k, m], sums)
        out_ref[0, m * unit:(m + 1) * unit, :] = sums[0] * F32(0.5)
        out_ref[1, m * unit:(m + 1) * unit, :] = sums[1] * keep

    pltpu.make_async_copy(recv, recv, rs).wait()

    @pl.loop(0, pieces)
    def _(k):
        near_copy(k).wait_send()

    for chunk in range(2):
        @pl.loop(0, pieces)
        def _(k):
            pass_copy(chunk, k).wait_send()


def local(n, amplitudes, integrals, c_index, d_index, a_index, b_index):
    _, block, depth = amplitudes.shape
    q = integrals.shape[1]
    rows = 4 * block // n
    unit = min(8, rows)
    pieces = depth // DEPTH
    dma = pltpu.SemaphoreType.DMA
    whole = pl.BlockSpec(memory_space=pltpu.VMEM)
    out = pl.pallas_call(
        functools.partial(kernel, n),
        out_shape=jax.ShapeDtypeStruct((2, rows, q), F32),
        in_specs=[pl.BlockSpec(memory_space=pl.ANY)] * 2 + [whole] * 4,
        out_specs=whole,
        scratch_shapes=[
            pltpu.VMEM((4, 2, block, depth), F32),
            pltpu.VMEM((depth, q), F32),
            pltpu.VMEM((depth, 2 * q), BF16),
            pltpu.VMEM((2, depth), F32),
            pltpu.VMEM((4 * (block - LAST), q), F32),
            pltpu.VMEM((4 * block, q), F32),
            pltpu.VMEM((4 * block // unit, 2, unit, q), F32),
            pltpu.VMEM((n - 1, rows // unit, 2, unit, q), F32),
            dma, dma((pieces,)), dma((pieces,)), dma((pieces,)),
            dma((2, pieces)), dma((2, pieces)), dma((2, pieces)), dma((2, pieces)), dma, dma,
        ],
        compiler_params=pltpu.CompilerParams(
            collective_id=0, has_side_effects=True, vmem_limit_bytes=56 * 1024 * 1024
        ),
        cost_estimate=pl.CostEstimate(
            flops=3 * 2 * 8 * block * depth * q,
            bytes_accessed=4 * depth * (q + 2 * block), transcendentals=0,
        ),
    )(amplitudes, integrals, c_index.reshape(1, -1), d_index.reshape(1, -1),
      a_index, b_index)
    return jnp.transpose(out, (1, 0, 2))


def solution(mesh):
    placed = (P(None, "ab", "cd"), P("cd", "ab"), P("cd"), P("cd"), P("ab"), P("ab"))
    return jax.shard_map(
        functools.partial(local, mesh.shape["cd"]), mesh=mesh, in_specs=placed,
        out_specs=P("cd", None, "ab"), check_vma=False,
    )
```

```python
import functools

import jax
import jax.numpy as jnp
from jax import lax
from jax.experimental import pallas as pl
from jax.experimental.pallas import tpu as pltpu
from jax.sharding import PartitionSpec as P

MESH = pl.DeviceIdType.MESH
BF16 = jnp.bfloat16
F32 = jnp.float32

LAST = 8
DEPTH = 1024


def split(x):
    high = x.astype(BF16)
    return high, (x - high.astype(F32)).astype(BF16)


def kernel(n, a_hbm, v_hbm, c_hbm, d_hbm, qa_hbm, qb_hbm, out_ref,
           held, v, v_split, weights, c_ref, d_ref, qa_ref, qb_ref, total, near, part, recv,
           own_sem, v_sem, index_sem, cs, cr, xs, xr, fs, fr, rs, rr):
    me = lax.axis_index("cd")
    j = lax.axis_index("ab")
    beside = j + 1 - 2 * lax.rem(j, 2)
    across = lax.rem(j + 2, 4)
    far = lax.rem(beside + 2, 4)
    block = a_hbm.shape[1]
    depth = a_hbm.shape[2]
    pieces = depth // DEPTH
    q = out_ref.shape[2]
    chunks = ((0, 2, block - LAST), (0, 1, LAST), (1, 1, LAST))

    def first_row(chunk, parity):
        return LAST * (1 - parity) if chunk == 0 else (block - LAST) * parity

    unit = part.shape[2]
    mine = recv.shape[1]

    barrier = pltpu.get_barrier_semaphore()
    for other in (beside, across):
        pl.semaphore_signal(barrier, inc=1, device_id={"ab": other}, device_id_type=MESH)

    @pl.loop(1, n)
    def _(step):
        pl.semaphore_signal(
            barrier, inc=1, device_id={"cd": lax.rem(me + step, n)}, device_id_type=MESH
        )

    own = pltpu.make_async_copy(a_hbm, held.at[0], own_sem)
    own.start()

    def v_copy(k):
        at = pl.ds(pl.multiple_of(k * DEPTH, DEPTH), DEPTH)
        return pltpu.make_async_copy(v_hbm.at[at], v.at[at], v_sem.at[k])

    @pl.loop(0, pieces)
    def _(k):
        v_copy(k).start()

    pl.semaphore_wait(barrier, n + 1)

    def columns(k):
        return pl.ds(pl.multiple_of(k * DEPTH, DEPTH), DEPTH)

    parity = lax.rem(j, 2)

    def window(chunk, k):
        slab, slabs, count = chunks[chunk]
        row = pl.multiple_of(first_row(chunk, parity), 8)
        return pl.ds(slab, slabs), pl.ds(row, count), columns(k)

    def cross_copy(chunk, k):
        at = window(chunk, k)
        return pltpu.make_async_remote_copy(
            src_ref=a_hbm.at[*at], dst_ref=held.at[2, *at],
            send_sem=xs.at[chunk, k], recv_sem=xr.at[chunk, k],
            device_id={"ab": across}, device_id_type=MESH,
        )

    def pass_copy(chunk, k):
        at = window(chunk, k)
        return pltpu.make_async_remote_copy(
            src_ref=held.at[2, *at], dst_ref=held.at[3, *at],
            send_sem=fs.at[chunk, k], recv_sem=fr.at[chunk, k],
            device_id={"ab": beside}, device_id_type=MESH,
        )

    def near_copy(k):
        cols = columns(k)
        return pltpu.make_async_remote_copy(
            src_ref=a_hbm.at[:, :, cols], dst_ref=held.at[1, :, :, cols],
            send_sem=cs.at[k], recv_sem=cr.at[k],
            device_id={"ab": beside}, device_id_type=MESH,
        )

    @pl.loop(0, pieces)
    def _(k):
        cross_copy(0, k).start()

    @pl.loop(0, pieces)
    def _(k):
        near_copy(k).start()

    index_copies = [
        pltpu.make_async_copy(src, dst, index_sem.at[i])
        for i, (src, dst) in enumerate(
            ((c_hbm, c_ref), (d_hbm, d_ref), (qa_hbm, qa_ref), (qb_hbm, qb_ref)))
    ]
    for copy in index_copies:
        copy.start()
    for copy in index_copies:
        copy.wait()
    same = c_ref[...] == d_ref[...]
    weights[0:1, :] = jnp.where(same, F32(0.5), F32(1.0))
    weights[1:2, :] = jnp.where(same, F32(0.0), F32(1.0))

    def product(cols, *operands):
        x = jnp.concatenate([
            held[slot, slab, rows, cols] * weights[slab:slab + 1, cols]
            for slot, slab, rows in operands
        ], axis=0)
        high, low = split(x)
        count = x.shape[0]
        out = jnp.dot(jnp.concatenate([high, low], axis=0), v_split[cols, :],
                      preferred_element_type=F32)
        return out[:count, :q] + (out[count:, :q] + out[:count, q:])

    def send_sums(row, sums):
        slabs = pl.ds(min(sums), len(sums))
        for m in range(8 // unit):
            message = row // unit + m
            for slab, value in sums.items():
                part[message, slab] = value[m * unit:(m + 1) * unit]
            owner = message // mine

            @pl.when(owner != me)
            def _():
                pltpu.make_async_remote_copy(
                    src_ref=part.at[message, slabs],
                    dst_ref=recv.at[lax.rem(me - owner - 1 + n, n), lax.rem(message, mine), slabs],
                    send_sem=rs, recv_sem=rr,
                    device_id={"cd": owner}, device_id_type=MESH,
                ).start()

    own.wait()
    near[...] = jnp.zeros_like(near)

    @pl.loop(0, pieces)
    def _(k):
        cols = columns(k)
        v_copy(k).wait()
        v_split[cols, :q], v_split[cols, q:] = split(v[cols, :])
        near_copy(k).wait_recv()
        near[...] += product(
            cols, *((slot, slab, pl.ds(0, block)) for slot in (0, 1) for slab in range(2)))

    for at, owner in ((0, j), (1, beside)):
        for row in range(0, block, 8):
            base = at * 2 * block + row
            send_sums(owner * block + row,
                      {s: near[base + s * block:base + s * block + 8, :] for s in range(2)})

    for chunk, (slab, slabs, count) in enumerate(chunks):
        blocks = ((2, across, parity), (3, far, 1 - parity))
        size = 2 * slabs * count
        total[:size, :] = jnp.zeros((size, q), F32)

        def add(k):
            pass_copy(chunk, k).wait_recv()
            total[:size, :] += product(columns(k), *(
                (slot, one, pl.ds(pl.multiple_of(first_row(chunk, odd), 8), count))
                for slot, _, odd in blocks for one in range(slab, slab + slabs)))

        @pl.loop(0, pieces)
        def _(k):
            cross_copy(chunk, k).wait_recv()
            pass_copy(chunk, k).start()
            cross_copy(chunk, k).wait_send()
            if chunk + 1 < len(chunks):
                cross_copy(chunk + 1, k).start()

            @pl.when(k > 0)
            def _():
                add(k - 1)

        add(pieces - 1)
        for at, (_, owner, odd) in enumerate(blocks):
            for row in range(0, count, 8):
                base = at * slabs * count + row
                send_sums(owner * block + first_row(chunk, odd) + row, {
                    slab + s: total[base + s * count:base + s * count + 8, :]
                    for s in range(slabs)})

    @pl.loop(0, pieces)
    def _(k):
        near_copy(k).wait_send()
        for chunk in range(len(chunks)):
            pass_copy(chunk, k).wait_send()

    keep = jnp.where(qa_ref[...] == qb_ref[...], F32(0.0), F32(0.5)).reshape(1, q)
    pltpu.make_async_copy(recv, recv, rr).wait()
    for m in range(mine):
        sums = part[me * mine + m]
        sums = lax.fori_loop(0, n - 1, lambda k, acc: acc + recv[k, m], sums)
        out_ref[0, m * unit:(m + 1) * unit, :] = sums[0] * F32(0.5)
        out_ref[1, m * unit:(m + 1) * unit, :] = sums[1] * keep

    pltpu.make_async_copy(recv, recv, rs).wait()


def local(n, amplitudes, integrals, c_index, d_index, a_index, b_index):
    _, block, depth = amplitudes.shape
    q = integrals.shape[1]
    rows = 4 * block // n
    unit = min(8, rows)
    pieces = depth // DEPTH
    dma = pltpu.SemaphoreType.DMA
    out = pl.pallas_call(
        functools.partial(kernel, n),
        out_shape=jax.ShapeDtypeStruct((2, rows, q), F32),
        in_specs=[pl.BlockSpec(memory_space=pl.ANY)] * 6,
        out_specs=pl.BlockSpec(memory_space=pltpu.VMEM),
        scratch_shapes=[
            pltpu.VMEM((4, 2, block, depth), F32),
            pltpu.VMEM((depth, q), F32),
            pltpu.VMEM((depth, 2 * q), BF16),
            pltpu.VMEM((2, depth), F32),
            pltpu.VMEM((1, depth), jnp.int32),
            pltpu.VMEM((1, depth), jnp.int32),
            pltpu.VMEM((q,), jnp.int32),
            pltpu.VMEM((q,), jnp.int32),
            pltpu.VMEM((4 * (block - LAST), q), F32),
            pltpu.VMEM((4 * block, q), F32),
            pltpu.VMEM((4 * block // unit, 2, unit, q), F32),
            pltpu.VMEM((n - 1, rows // unit, 2, unit, q), F32),
            dma, dma((pieces,)), dma((4,)), dma((pieces,)), dma((pieces,)),
            dma((3, pieces)), dma((3, pieces)), dma((3, pieces)), dma((3, pieces)), dma, dma,
        ],
        compiler_params=pltpu.CompilerParams(
            collective_id=0, has_side_effects=True, vmem_limit_bytes=56 * 1024 * 1024
        ),
        cost_estimate=pl.CostEstimate(
            flops=3 * 2 * 8 * block * depth * q,
            bytes_accessed=4 * depth * (q + 2 * block), transcendentals=0,
        ),
    )(amplitudes, integrals, c_index.reshape(1, -1), d_index.reshape(1, -1),
      a_index, b_index)
    return jnp.transpose(out, (1, 0, 2))


def solution(mesh):
    placed = (P(None, "ab", "cd"), P("cd", "ab"), P("cd"), P("cd"), P("ab"), P("ab"))
    return jax.shard_map(
        functools.partial(local, mesh.shape["cd"]), mesh=mesh, in_specs=placed,
        out_specs=P("cd", None, "ab"), check_vma=False,
    )
```

```python
import functools

import jax
import jax.numpy as jnp
from jax import lax
from jax.experimental import pallas as pl
from jax.experimental.pallas import tpu as pltpu
from jax.sharding import PartitionSpec as P

MESH = pl.DeviceIdType.MESH
BF16 = jnp.bfloat16
F32 = jnp.float32

LAST = 8
DEPTH = 1024


def split(x):
    high = x.astype(BF16)
    return high, (x - high.astype(F32)).astype(BF16)


def kernel(n, a_hbm, v_hbm, c_hbm, d_hbm, qa_hbm, qb_hbm, out_ref,
           held, v, v_split, weights, c_ref, d_ref, qa_ref, qb_ref, total, near, part, recv,
           own_sem, v_sem, index_sem, cs, cr, xs, xr, fs, fr, rs, rr):
    me = lax.axis_index("cd")
    j = lax.axis_index("ab")
    beside = j + 1 - 2 * lax.rem(j, 2)
    across = lax.rem(j + 2, 4)
    far = lax.rem(beside + 2, 4)
    block = a_hbm.shape[1]
    depth = a_hbm.shape[2]
    pieces = depth // DEPTH
    q = out_ref.shape[2]
    chunks = (block - LAST, LAST)

    def first_row(chunk, parity):
        return LAST * (1 - parity) if chunk == 0 else (block - LAST) * parity

    unit = part.shape[2]
    mine = recv.shape[1]

    barrier = pltpu.get_barrier_semaphore()
    for other in (beside, across):
        pl.semaphore_signal(barrier, inc=1, device_id={"ab": other}, device_id_type=MESH)

    @pl.loop(1, n)
    def _(step):
        pl.semaphore_signal(
            barrier, inc=1, device_id={"cd": lax.rem(me + step, n)}, device_id_type=MESH
        )

    own = pltpu.make_async_copy(a_hbm, held.at[0], own_sem)
    own.start()

    def v_copy(k):
        at = pl.ds(pl.multiple_of(k * DEPTH, DEPTH), DEPTH)
        return pltpu.make_async_copy(v_hbm.at[at], v.at[at], v_sem.at[k])

    @pl.loop(0, pieces)
    def _(k):
        v_copy(k).start()

    pl.semaphore_wait(barrier, n + 1)

    def columns(k):
        return pl.ds(pl.multiple_of(k * DEPTH, DEPTH), DEPTH)

    parity = lax.rem(j, 2)

    def window(chunk, k):
        row = pl.multiple_of(first_row(chunk, parity), 8)
        return slice(None), pl.ds(row, chunks[chunk]), columns(k)

    def cross_copy(chunk, k):
        at = window(chunk, k)
        return pltpu.make_async_remote_copy(
            src_ref=a_hbm.at[*at], dst_ref=held.at[2, *at],
            send_sem=xs.at[chunk, k], recv_sem=xr.at[chunk, k],
            device_id={"ab": across}, device_id_type=MESH,
        )

    def pass_copy(chunk, k):
        at = window(chunk, k)
        return pltpu.make_async_remote_copy(
            src_ref=held.at[2, *at], dst_ref=held.at[3, *at],
            send_sem=fs.at[chunk, k], recv_sem=fr.at[chunk, k],
            device_id={"ab": beside}, device_id_type=MESH,
        )

    def near_copy(k):
        cols = columns(k)
        return pltpu.make_async_remote_copy(
            src_ref=a_hbm.at[:, :, cols], dst_ref=held.at[1, :, :, cols],
            send_sem=cs.at[k], recv_sem=cr.at[k],
            device_id={"ab": beside}, device_id_type=MESH,
        )

    @pl.loop(0, pieces)
    def _(k):
        cross_copy(0, k).start()

    @pl.loop(0, pieces)
    def _(k):
        near_copy(k).start()

    index_copies = [
        pltpu.make_async_copy(src, dst, index_sem.at[i])
        for i, (src, dst) in enumerate(
            ((c_hbm, c_ref), (d_hbm, d_ref), (qa_hbm, qa_ref), (qb_hbm, qb_ref)))
    ]
    for copy in index_copies:
        copy.start()
    for copy in index_copies:
        copy.wait()
    same = c_ref[...] == d_ref[...]
    weights[0:1, :] = jnp.where(same, F32(0.5), F32(1.0))
    weights[1:2, :] = jnp.where(same, F32(0.0), F32(1.0))

    def product(cols, *operands):
        x = jnp.concatenate([
            held[slot, slab, rows, cols] * weights[slab:slab + 1, cols]
            for slot, slab, rows in operands
        ], axis=0)
        high, low = split(x)
        count = x.shape[0]
        out = jnp.dot(jnp.concatenate([high, low], axis=0), v_split[cols, :],
                      preferred_element_type=F32)
        return out[:count, :q] + (out[count:, :q] + out[:count, q:])

    def send_sums(sums, at, row, count):
        @pl.loop(0, count, step=8)
        def _(done):
            values = [sums[pl.ds(pl.multiple_of(at + s * count + done, 8), 8), :]
                      for s in range(2)]
            for m in range(8 // unit):
                message = (row + done) // unit + m
                for s in range(2):
                    part[message, s] = values[s][m * unit:(m + 1) * unit]
                owner = message // mine

                @pl.when(owner != me)
                def _():
                    slot = lax.rem(me - owner - 1 + n, n)
                    pltpu.make_async_remote_copy(
                        src_ref=part.at[message], dst_ref=recv.at[slot, lax.rem(message, mine)],
                        send_sem=rs, recv_sem=rr,
                        device_id={"cd": owner}, device_id_type=MESH,
                    ).start()

    own.wait()
    near[...] = jnp.zeros_like(near)

    @pl.loop(0, pieces)
    def _(k):
        cols = columns(k)
        v_copy(k).wait()
        v_split[cols, :q], v_split[cols, q:] = split(v[cols, :])
        near_copy(k).wait_recv()
        near[...] += product(
            cols, *((slot, slab, pl.ds(0, block)) for slot in (0, 1) for slab in range(2)))

    for at, owner in ((0, j), (1, beside)):
        send_sums(near, at * 2 * block, owner * block, block)

    for chunk, count in enumerate(chunks):
        blocks = ((2, across, parity), (3, far, 1 - parity))
        size = 4 * count
        total[:size, :] = jnp.zeros((size, q), F32)

        def add(k):
            pass_copy(chunk, k).wait_recv()
            total[:size, :] += product(columns(k), *(
                (slot, slab, pl.ds(pl.multiple_of(first_row(chunk, odd), 8), count))
                for slot, _, odd in blocks for slab in range(2)))

        @pl.loop(0, pieces)
        def _(k):
            cross_copy(chunk, k).wait_recv()
            pass_copy(chunk, k).start()
            cross_copy(chunk, k).wait_send()
            if chunk == 0:
                cross_copy(1, k).start()

            @pl.when(k > 0)
            def _():
                add(k - 1)

        add(pieces - 1)
        for at, (_, owner, odd) in enumerate(blocks):
            send_sums(total, at * 2 * count, owner * block + first_row(chunk, odd), count)

    @pl.loop(0, pieces)
    def _(k):
        near_copy(k).wait_send()
        for chunk in range(len(chunks)):
            pass_copy(chunk, k).wait_send()

    keep = jnp.where(qa_ref[...] == qb_ref[...], F32(0.0), F32(0.5)).reshape(1, q)
    pltpu.make_async_copy(recv, recv, rr).wait()
    for m in range(mine):
        sums = part[me * mine + m]
        sums = lax.fori_loop(0, n - 1, lambda k, acc: acc + recv[k, m], sums)
        out_ref[0, m * unit:(m + 1) * unit, :] = sums[0] * F32(0.5)
        out_ref[1, m * unit:(m + 1) * unit, :] = sums[1] * keep

    pltpu.make_async_copy(recv, recv, rs).wait()


def local(n, amplitudes, integrals, c_index, d_index, a_index, b_index):
    _, block, depth = amplitudes.shape
    q = integrals.shape[1]
    rows = 4 * block // n
    unit = min(8, rows)
    pieces = depth // DEPTH
    dma = pltpu.SemaphoreType.DMA
    out = pl.pallas_call(
        functools.partial(kernel, n),
        out_shape=jax.ShapeDtypeStruct((2, rows, q), F32),
        in_specs=[pl.BlockSpec(memory_space=pltpu.HBM)] * 6,
        out_specs=pl.BlockSpec(memory_space=pltpu.VMEM),
        scratch_shapes=[
            pltpu.VMEM((4, 2, block, depth), F32),
            pltpu.VMEM((depth, q), F32),
            pltpu.VMEM((depth, 2 * q), BF16),
            pltpu.VMEM((2, depth), F32),
            pltpu.VMEM((1, depth), jnp.int32),
            pltpu.VMEM((1, depth), jnp.int32),
            pltpu.VMEM((q,), jnp.int32),
            pltpu.VMEM((q,), jnp.int32),
            pltpu.VMEM((4 * (block - LAST), q), F32),
            pltpu.VMEM((4 * block, q), F32),
            pltpu.VMEM((4 * block // unit, 2, unit, q), F32),
            pltpu.VMEM((n - 1, rows // unit, 2, unit, q), F32),
            dma, dma((pieces,)), dma((4,)), dma((pieces,)), dma((pieces,)),
            dma((2, pieces)), dma((2, pieces)), dma((2, pieces)), dma((2, pieces)), dma, dma,
        ],
        compiler_params=pltpu.CompilerParams(
            collective_id=0, has_side_effects=True, vmem_limit_bytes=44 * 1024 * 1024
        ),
        cost_estimate=pl.CostEstimate(
            flops=3 * 2 * 8 * block * depth * q,
            bytes_accessed=4 * depth * (q + 2 * block), transcendentals=0,
        ),
    )(*(pltpu.with_memory_space_constraint(x, pltpu.HBM) for x in (
        amplitudes, integrals, c_index.reshape(1, -1), d_index.reshape(1, -1), a_index, b_index)))
    return jnp.transpose(out, (1, 0, 2))


def solution(mesh):
    placed = (P(None, "ab", "cd"), P("cd", "ab"), P("cd"), P("cd"), P("ab"), P("ab"))
    return jax.shard_map(
        functools.partial(local, mesh.shape["cd"]), mesh=mesh, in_specs=placed,
        out_specs=P("cd", None, "ab"), check_vma=False,
    )
```

```python
import functools

import jax
import jax.numpy as jnp
from jax import lax
from jax.experimental import pallas as pl
from jax.experimental.pallas import tpu as pltpu
from jax.sharding import PartitionSpec as P

MESH = pl.DeviceIdType.MESH
BF16 = jnp.bfloat16
F32 = jnp.float32

LAST = 8
DEPTH = 1024


def split(x):
    high = x.astype(BF16)
    return high, (x - high.astype(F32)).astype(BF16)


def kernel(n, a_hbm, v_hbm, c_hbm, d_hbm, qa_hbm, qb_hbm, out_ref,
           held, v, v_split, weights, c_ref, d_ref, qa_ref, qb_ref, total, near, part, recv,
           own_sem, v_sem, index_sem, cs, cr, xs, xr, fs, fr, rs, rr):
    me = lax.axis_index("cd")
    j = lax.axis_index("ab")
    beside = j + 1 - 2 * lax.rem(j, 2)
    across = lax.rem(j + 2, 4)
    far = lax.rem(beside + 2, 4)
    block = a_hbm.shape[1]
    depth = a_hbm.shape[2]
    pieces = depth // DEPTH
    q = out_ref.shape[2]
    groups = ((0, 2, block - LAST), (0, 1, LAST), (1, 1, LAST))
    chunks = ((0, 1), (2,))

    def first_row(group, parity):
        row = LAST * (1 - parity) if group == 0 else (block - LAST) * parity
        return pl.multiple_of(row, 8)

    unit = part.shape[2]
    mine = recv.shape[1]

    barrier = pltpu.get_barrier_semaphore()
    for other in (beside, across):
        pl.semaphore_signal(barrier, inc=1, device_id={"ab": other}, device_id_type=MESH)

    @pl.loop(1, n)
    def _(step):
        pl.semaphore_signal(
            barrier, inc=1, device_id={"cd": lax.rem(me + step, n)}, device_id_type=MESH
        )

    own = pltpu.make_async_copy(a_hbm, held.at[0], own_sem)
    own.start()

    def v_copy(k):
        at = pl.ds(pl.multiple_of(k * DEPTH, DEPTH), DEPTH)
        return pltpu.make_async_copy(v_hbm.at[at], v.at[at], v_sem.at[k])

    @pl.loop(0, pieces)
    def _(k):
        v_copy(k).start()

    pl.semaphore_wait(barrier, n + 1)

    def columns(k):
        return pl.ds(pl.multiple_of(k * DEPTH, DEPTH), DEPTH)

    parity = lax.rem(j, 2)

    def window(group, k):
        slab, slabs, count = groups[group]
        return pl.ds(slab, slabs), pl.ds(first_row(group, parity), count), columns(k)

    def cross_copy(group, k):
        at = window(group, k)
        return pltpu.make_async_remote_copy(
            src_ref=a_hbm.at[*at], dst_ref=held.at[2, *at],
            send_sem=xs.at[group, k], recv_sem=xr.at[group, k],
            device_id={"ab": across}, device_id_type=MESH,
        )

    def pass_copy(group, k):
        at = window(group, k)
        return pltpu.make_async_remote_copy(
            src_ref=held.at[2, *at], dst_ref=held.at[3, *at],
            send_sem=fs.at[group, k], recv_sem=fr.at[group, k],
            device_id={"ab": beside}, device_id_type=MESH,
        )

    def near_copy(k):
        cols = columns(k)
        return pltpu.make_async_remote_copy(
            src_ref=a_hbm.at[:, :, cols], dst_ref=held.at[1, :, :, cols],
            send_sem=cs.at[k], recv_sem=cr.at[k],
            device_id={"ab": beside}, device_id_type=MESH,
        )

    @pl.loop(0, pieces)
    def _(k):
        for group in chunks[0]:
            cross_copy(group, k).start()

    @pl.loop(0, pieces)
    def _(k):
        near_copy(k).start()

    index_copies = [
        pltpu.make_async_copy(src, dst, index_sem.at[i])
        for i, (src, dst) in enumerate(
            ((c_hbm, c_ref), (d_hbm, d_ref), (qa_hbm, qa_ref), (qb_hbm, qb_ref)))
    ]
    for copy in index_copies:
        copy.start()
    for copy in index_copies:
        copy.wait()
    same = c_ref[...] == d_ref[...]
    weights[0:1, :] = jnp.where(same, F32(0.5), F32(1.0))
    weights[1:2, :] = jnp.where(same, F32(0.0), F32(1.0))

    def product(cols, *operands):
        x = jnp.concatenate([
            held[slot, slab, rows, cols] * weights[slab:slab + 1, cols]
            for slot, slab, rows in operands
        ], axis=0)
        high, low = split(x)
        count = x.shape[0]
        out = jnp.dot(jnp.concatenate([high, low], axis=0), v_split[cols, :],
                      preferred_element_type=F32)
        return out[:count, :q] + (out[count:, :q] + out[:count, q:])

    def send_sums(sums, at, row, slab, slabs, count):
        these = pl.ds(slab, slabs)

        @pl.loop(0, count, step=8)
        def _(done):
            values = [sums[pl.ds(pl.multiple_of(at + s * count + done, 8), 8), :]
                      for s in range(slabs)]
            for m in range(8 // unit):
                message = (row + done) // unit + m
                for s in range(slabs):
                    part[message, slab + s] = values[s][m * unit:(m + 1) * unit]
                owner = message // mine

                @pl.when(owner != me)
                def _():
                    slot = lax.rem(me - owner - 1 + n, n)
                    pltpu.make_async_remote_copy(
                        src_ref=part.at[message, these],
                        dst_ref=recv.at[slot, lax.rem(message, mine), these],
                        send_sem=rs, recv_sem=rr,
                        device_id={"cd": owner}, device_id_type=MESH,
                    ).start()

    own.wait()
    near[...] = jnp.zeros_like(near)

    @pl.loop(0, pieces)
    def _(k):
        cols = columns(k)
        v_copy(k).wait()
        v_split[cols, :q], v_split[cols, q:] = split(v[cols, :])
        near_copy(k).wait_recv()
        near[...] += product(
            cols, *((slot, slab, pl.ds(0, block)) for slot in (0, 1) for slab in range(2)))

    for at, owner in ((0, j), (1, beside)):
        send_sums(near, at * 2 * block, owner * block, 0, 2, block)

    for chunk in chunks:
        blocks = ((2, across, parity), (3, far, 1 - parity))
        size = sum(2 * groups[group][1] * groups[group][2] for group in chunk)
        total[:size, :] = jnp.zeros((size, q), F32)

        def add(k):
            for group in chunk:
                pass_copy(group, k).wait_recv()
            total[:size, :] += product(columns(k), *(
                (slot, slab + s, pl.ds(first_row(group, odd), count))
                for group in chunk for slab, slabs, count in (groups[group],)
                for slot, _, odd in blocks for s in range(slabs)))

        @pl.loop(0, pieces)
        def _(k):
            for group in chunk:
                cross_copy(group, k).wait_recv()
                pass_copy(group, k).start()
            if chunk == chunks[0]:
                for group in chunk:
                    cross_copy(group, k).wait_send()
                for group in chunks[1]:
                    cross_copy(group, k).start()

            @pl.when(k > 0)
            def _():
                add(k - 1)

        add(pieces - 1)
        at = 0
        for group in chunk:
            slab, slabs, count = groups[group]
            for _, owner, odd in blocks:
                send_sums(total, at, owner * block + first_row(group, odd), slab, slabs, count)
                at += slabs * count

    @pl.loop(0, pieces)
    def _(k):
        near_copy(k).wait_send()
        for group in range(len(groups)):
            pass_copy(group, k).wait_send()
        for group in chunks[1]:
            cross_copy(group, k).wait_send()

    keep = jnp.where(qa_ref[...] == qb_ref[...], F32(0.0), F32(0.5)).reshape(1, q)
    pltpu.make_async_copy(recv, recv, rr).wait()
    for m in range(mine):
        sums = part[me * mine + m]
        sums = lax.fori_loop(0, n - 1, lambda k, acc: acc + recv[k, m], sums)
        out_ref[0, m * unit:(m + 1) * unit, :] = sums[0] * F32(0.5)
        out_ref[1, m * unit:(m + 1) * unit, :] = sums[1] * keep

    pltpu.make_async_copy(recv, recv, rs).wait()


def local(n, amplitudes, integrals, c_index, d_index, a_index, b_index):
    _, block, depth = amplitudes.shape
    q = integrals.shape[1]
    rows = 4 * block // n
    unit = min(8, rows)
    pieces = depth // DEPTH
    dma = pltpu.SemaphoreType.DMA
    out = pl.pallas_call(
        functools.partial(kernel, n),
        out_shape=jax.ShapeDtypeStruct((2, rows, q), F32),
        in_specs=[pl.BlockSpec(memory_space=pltpu.HBM)] * 6,
        out_specs=pl.BlockSpec(memory_space=pltpu.VMEM),
        scratch_shapes=[
            pltpu.VMEM((4, 2, block, depth), F32),
            pltpu.VMEM((depth, q), F32),
            pltpu.VMEM((depth, 2 * q), BF16),
            pltpu.VMEM((2, depth), F32),
            pltpu.VMEM((1, depth), jnp.int32),
            pltpu.VMEM((1, depth), jnp.int32),
            pltpu.VMEM((q,), jnp.int32),
            pltpu.VMEM((q,), jnp.int32),
            pltpu.VMEM((4 * block, q), F32),
            pltpu.VMEM((4 * block, q), F32),
            pltpu.VMEM((4 * block // unit, 2, unit, q), F32),
            pltpu.VMEM((n - 1, rows // unit, 2, unit, q), F32),
            dma, dma((pieces,)), dma((4,)), dma((pieces,)), dma((pieces,)),
            dma((3, pieces)), dma((3, pieces)), dma((3, pieces)), dma((3, pieces)), dma, dma,
        ],
        compiler_params=pltpu.CompilerParams(
            collective_id=0, has_side_effects=True, vmem_limit_bytes=44 * 1024 * 1024
        ),
        cost_estimate=pl.CostEstimate(
            flops=3 * 2 * 8 * block * depth * q,
            bytes_accessed=4 * depth * (q + 2 * block), transcendentals=0,
        ),
    )(*(pltpu.with_memory_space_constraint(x, pltpu.HBM) for x in (
        amplitudes, integrals, c_index.reshape(1, -1), d_index.reshape(1, -1), a_index, b_index)))
    return jnp.transpose(out, (1, 0, 2))


def solution(mesh):
    placed = (P(None, "ab", "cd"), P("cd", "ab"), P("cd"), P("cd"), P("ab"), P("ab"))
    return jax.shard_map(
        functools.partial(local, mesh.shape["cd"]), mesh=mesh, in_specs=placed,
        out_specs=P("cd", None, "ab"), check_vma=False,
    )
```

```python
import functools

import jax
import jax.numpy as jnp
from jax import lax
from jax.experimental import pallas as pl
from jax.experimental.pallas import tpu as pltpu
from jax.sharding import PartitionSpec as P

MESH = pl.DeviceIdType.MESH
BF16 = jnp.bfloat16
F32 = jnp.float32

LAST = 8
DEPTH = 1024
LAG = 1


def split(x):
    high = x.astype(BF16)
    return high, (x - high.astype(F32)).astype(BF16)


def kernel(n, a_hbm, v_hbm, c_hbm, d_hbm, qa_hbm, qb_hbm, out_ref,
           held, v, v_split, weights, c_ref, d_ref, qa_ref, qb_ref, total, near, part, recv,
           own_sem, v_sem, index_sem, cs, cr, xs, xr, fs, fr, rs, rr):
    me = lax.axis_index("cd")
    j = lax.axis_index("ab")
    beside = j + 1 - 2 * lax.rem(j, 2)
    across = lax.rem(j + 2, 4)
    far = lax.rem(beside + 2, 4)
    block = a_hbm.shape[1]
    depth = a_hbm.shape[2]
    pieces = depth // DEPTH
    q = out_ref.shape[2]
    groups = ((0, 2, block - LAST), (0, 2, LAST))
    chunks = ((0,), (1,))

    def first_row(group, parity):
        row = LAST * (1 - parity) if group == 0 else (block - LAST) * parity
        return pl.multiple_of(row, 8)

    unit = part.shape[2]
    mine = recv.shape[1]

    barrier = pltpu.get_barrier_semaphore()
    for other in (beside, across):
        pl.semaphore_signal(barrier, inc=1, device_id={"ab": other}, device_id_type=MESH)

    @pl.loop(1, n)
    def _(step):
        pl.semaphore_signal(
            barrier, inc=1, device_id={"cd": lax.rem(me + step, n)}, device_id_type=MESH
        )

    own = pltpu.make_async_copy(a_hbm, held.at[0], own_sem)
    own.start()

    def v_copy(k):
        at = pl.ds(pl.multiple_of(k * DEPTH, DEPTH), DEPTH)
        return pltpu.make_async_copy(v_hbm.at[at], v.at[at], v_sem.at[k])

    @pl.loop(0, pieces)
    def _(k):
        v_copy(k).start()

    pl.semaphore_wait(barrier, n + 1)

    def columns(k):
        return pl.ds(pl.multiple_of(k * DEPTH, DEPTH), DEPTH)

    parity = lax.rem(j, 2)

    def window(group, k):
        slab, slabs, count = groups[group]
        return pl.ds(slab, slabs), pl.ds(first_row(group, parity), count), columns(k)

    def cross_copy(group, k):
        at = window(group, k)
        return pltpu.make_async_remote_copy(
            src_ref=a_hbm.at[*at], dst_ref=held.at[2, *at],
            send_sem=xs.at[group, k], recv_sem=xr.at[group, k],
            device_id={"ab": across}, device_id_type=MESH,
        )

    def pass_copy(group, k):
        at = window(group, k)
        return pltpu.make_async_remote_copy(
            src_ref=held.at[2, *at], dst_ref=held.at[3, *at],
            send_sem=fs.at[group, k], recv_sem=fr.at[group, k],
            device_id={"ab": beside}, device_id_type=MESH,
        )

    def near_copy(k):
        cols = columns(k)
        return pltpu.make_async_remote_copy(
            src_ref=a_hbm.at[:, :, cols], dst_ref=held.at[1, :, :, cols],
            send_sem=cs.at[k], recv_sem=cr.at[k],
            device_id={"ab": beside}, device_id_type=MESH,
        )

    @pl.loop(0, pieces)
    def _(k):
        for group in chunks[0]:
            cross_copy(group, k).start()

    @pl.loop(0, pieces)
    def _(k):
        near_copy(k).start()

    index_copies = [
        pltpu.make_async_copy(src, dst, index_sem.at[i])
        for i, (src, dst) in enumerate(
            ((c_hbm, c_ref), (d_hbm, d_ref), (qa_hbm, qa_ref), (qb_hbm, qb_ref)))
    ]
    for copy in index_copies:
        copy.start()
    for copy in index_copies:
        copy.wait()
    same = c_ref[...] == d_ref[...]
    weights[0:1, :] = jnp.where(same, F32(0.5), F32(1.0))
    weights[1:2, :] = jnp.where(same, F32(0.0), F32(1.0))

    def product(cols, *operands):
        x = jnp.concatenate([
            held[slot, slab, rows, cols] * weights[slab:slab + 1, cols]
            for slot, slab, rows in operands
        ], axis=0)
        high, low = split(x)
        count = x.shape[0]
        out = jnp.dot(jnp.concatenate([high, low], axis=0), v_split[cols, :],
                      preferred_element_type=F32)
        return out[:count, :q] + (out[count:, :q] + out[:count, q:])

    def send_sums(sums, at, row, slab, slabs, count):
        these = pl.ds(slab, slabs)

        @pl.loop(0, count, step=8)
        def _(done):
            values = [sums[pl.ds(pl.multiple_of(at + s * count + done, 8), 8), :]
                      for s in range(slabs)]
            for m in range(8 // unit):
                message = (row + done) // unit + m
                for s in range(slabs):
                    part[message, slab + s] = values[s][m * unit:(m + 1) * unit]
                owner = message // mine

                @pl.when(owner != me)
                def _():
                    slot = lax.rem(me - owner - 1 + n, n)
                    pltpu.make_async_remote_copy(
                        src_ref=part.at[message, these],
                        dst_ref=recv.at[slot, lax.rem(message, mine), these],
                        send_sem=rs, recv_sem=rr,
                        device_id={"cd": owner}, device_id_type=MESH,
                    ).start()

    own.wait()
    near[...] = jnp.zeros_like(near)

    @pl.loop(0, pieces)
    def _(k):
        cols = columns(k)
        v_copy(k).wait()
        v_split[cols, :q], v_split[cols, q:] = split(v[cols, :])
        near_copy(k).wait_recv()
        near[...] += product(
            cols, *((slot, slab, pl.ds(0, block)) for slot in (0, 1) for slab in range(2)))

    for at, owner in ((0, j), (1, beside)):
        send_sums(near, at * 2 * block, owner * block, 0, 2, block)

    blocks = ((2, across, parity), (3, far, 1 - parity))

    def forward(chunk, k):
        for group in chunk:
            cross_copy(group, k).wait_recv()
            pass_copy(group, k).start()
        if chunk == chunks[0]:
            for group in chunk:
                cross_copy(group, k).wait_send()
            for group in chunks[1]:
                cross_copy(group, k).start()

    def clear(chunk):
        size = sum(2 * groups[group][1] * groups[group][2] for group in chunk)
        total[:size, :] = jnp.zeros((size, q), F32)

    def add(chunk, k):
        for group in chunk:
            pass_copy(group, k).wait_recv()
        found = product(columns(k), *(
            (slot, slab + s, pl.ds(first_row(group, odd), count))
            for group in chunk for slab, slabs, count in (groups[group],)
            for slot, _, odd in blocks for s in range(slabs)))
        total[:found.shape[0], :] += found

    def finish(chunk):
        at = 0
        for group in chunk:
            slab, slabs, count = groups[group]
            for _, owner, odd in blocks:
                send_sums(total, at, owner * block + first_row(group, odd), slab, slabs, count)
                at += slabs * count

    clear(chunks[0])

    @pl.loop(0, pieces + LAG)
    def _(t):
        @pl.when(t < pieces)
        def _():
            forward(chunks[0], t)

        @pl.when(t >= pieces)
        def _():
            forward(chunks[1], t - pieces)

        @pl.when(t >= LAG)
        def _():
            add(chunks[0], t - LAG)

    finish(chunks[0])
    clear(chunks[1])

    @pl.loop(LAG, pieces + LAG)
    def _(t):
        @pl.when(t < pieces)
        def _():
            forward(chunks[1], t)

        add(chunks[1], t - LAG)

    finish(chunks[1])

    @pl.loop(0, pieces)
    def _(k):
        near_copy(k).wait_send()
        for group in range(len(groups)):
            pass_copy(group, k).wait_send()
        for group in chunks[1]:
            cross_copy(group, k).wait_send()

    keep = jnp.where(qa_ref[...] == qb_ref[...], F32(0.0), F32(0.5)).reshape(1, q)
    pltpu.make_async_copy(recv, recv, rr).wait()
    for m in range(mine):
        sums = part[me * mine + m]
        sums = lax.fori_loop(0, n - 1, lambda k, acc: acc + recv[k, m], sums)
        out_ref[0, m * unit:(m + 1) * unit, :] = sums[0] * F32(0.5)
        out_ref[1, m * unit:(m + 1) * unit, :] = sums[1] * keep

    pltpu.make_async_copy(recv, recv, rs).wait()


def local(n, amplitudes, integrals, c_index, d_index, a_index, b_index):
    _, block, depth = amplitudes.shape
    q = integrals.shape[1]
    rows = 4 * block // n
    unit = min(8, rows)
    pieces = depth // DEPTH
    dma = pltpu.SemaphoreType.DMA
    out = pl.pallas_call(
        functools.partial(kernel, n),
        out_shape=jax.ShapeDtypeStruct((2, rows, q), F32),
        in_specs=[pl.BlockSpec(memory_space=pltpu.HBM)] * 6,
        out_specs=pl.BlockSpec(memory_space=pltpu.VMEM),
        scratch_shapes=[
            pltpu.VMEM((4, 2, block, depth), F32),
            pltpu.VMEM((depth, q), F32),
            pltpu.VMEM((depth, 2 * q), BF16),
            pltpu.VMEM((2, depth), F32),
            pltpu.VMEM((1, depth), jnp.int32),
            pltpu.VMEM((1, depth), jnp.int32),
            pltpu.VMEM((q,), jnp.int32),
            pltpu.VMEM((q,), jnp.int32),
            pltpu.VMEM((4 * block, q), F32),
            pltpu.VMEM((4 * block, q), F32),
            pltpu.VMEM((4 * block // unit, 2, unit, q), F32),
            pltpu.VMEM((n - 1, rows // unit, 2, unit, q), F32),
            dma, dma((pieces,)), dma((4,)), dma((pieces,)), dma((pieces,)),
            dma((2, pieces)), dma((2, pieces)), dma((2, pieces)), dma((2, pieces)), dma, dma,
        ],
        compiler_params=pltpu.CompilerParams(
            collective_id=0, has_side_effects=True, vmem_limit_bytes=44 * 1024 * 1024
        ),
        cost_estimate=pl.CostEstimate(
            flops=3 * 2 * 8 * block * depth * q,
            bytes_accessed=4 * depth * (q + 2 * block), transcendentals=0,
        ),
    )(*(pltpu.with_memory_space_constraint(x, pltpu.HBM) for x in (
        amplitudes, integrals, c_index.reshape(1, -1), d_index.reshape(1, -1), a_index, b_index)))
    return jnp.transpose(out, (1, 0, 2))


def solution(mesh):
    placed = (P(None, "ab", "cd"), P("cd", "ab"), P("cd"), P("cd"), P("ab"), P("ab"))
    return jax.shard_map(
        functools.partial(local, mesh.shape["cd"]), mesh=mesh, in_specs=placed,
        out_specs=P("cd", None, "ab"), check_vma=False,
    )
```

```python
import functools

import jax
import jax.numpy as jnp
from jax import lax
from jax.experimental import pallas as pl
from jax.experimental.pallas import tpu as pltpu
from jax.sharding import PartitionSpec as P

MESH = pl.DeviceIdType.MESH
BF16 = jnp.bfloat16
F32 = jnp.float32

LAST = 8
DEPTH = 1024
LAG = 1
AHEAD = 3
EARLY = 2


def split(x):
    high = x.astype(BF16)
    return high, (x - high.astype(F32)).astype(BF16)


def kernel(n, a_hbm, v_hbm, c_hbm, d_hbm, qa_hbm, qb_hbm, out_ref,
           held, v, v_split, weights, c_ref, d_ref, qa_ref, qb_ref, total, near, part, recv,
           own_sem, v_sem, index_sem, cs, cr, xs, xr, fs, fr, rs, rr):
    me = lax.axis_index("cd")
    j = lax.axis_index("ab")
    beside = j + 1 - 2 * lax.rem(j, 2)
    across = lax.rem(j + 2, 4)
    far = lax.rem(beside + 2, 4)
    block = a_hbm.shape[1]
    depth = a_hbm.shape[2]
    pieces = depth // DEPTH
    q = out_ref.shape[2]
    groups = ((0, 2, block - LAST), (0, 2, LAST))
    chunks = ((0,), (1,))

    def first_row(group, parity):
        row = LAST * (1 - parity) if group == 0 else (block - LAST) * parity
        return pl.multiple_of(row, 8)

    unit = part.shape[2]
    mine = recv.shape[1]

    barrier = pltpu.get_barrier_semaphore()
    for other in (beside, across):
        pl.semaphore_signal(barrier, inc=1, device_id={"ab": other}, device_id_type=MESH)

    @pl.loop(1, n)
    def _(step):
        pl.semaphore_signal(
            barrier, inc=1, device_id={"cd": lax.rem(me + step, n)}, device_id_type=MESH
        )

    own = pltpu.make_async_copy(a_hbm, held.at[0], own_sem)
    own.start()

    def v_copy(k):
        at = pl.ds(pl.multiple_of(k * DEPTH, DEPTH), DEPTH)
        return pltpu.make_async_copy(v_hbm.at[at], v.at[at], v_sem.at[k])

    @pl.loop(0, pieces)
    def _(k):
        v_copy(k).start()

    pl.semaphore_wait(barrier, n + 1)

    def columns(k):
        return pl.ds(pl.multiple_of(k * DEPTH, DEPTH), DEPTH)

    parity = lax.rem(j, 2)

    def window(group, k):
        slab, slabs, count = groups[group]
        return pl.ds(slab, slabs), pl.ds(first_row(group, parity), count), columns(k)

    def cross_copy(group, k):
        at = window(group, k)
        return pltpu.make_async_remote_copy(
            src_ref=a_hbm.at[*at], dst_ref=held.at[2, *at],
            send_sem=xs.at[group, k], recv_sem=xr.at[group, k],
            device_id={"ab": across}, device_id_type=MESH,
        )

    def pass_copy(group, k):
        at = window(group, k)
        return pltpu.make_async_remote_copy(
            src_ref=held.at[2, *at], dst_ref=held.at[3, *at],
            send_sem=fs.at[group, k], recv_sem=fr.at[group, k],
            device_id={"ab": beside}, device_id_type=MESH,
        )

    def near_copy(k):
        cols = columns(k)
        return pltpu.make_async_remote_copy(
            src_ref=a_hbm.at[:, :, cols], dst_ref=held.at[1, :, :, cols],
            send_sem=cs.at[k], recv_sem=cr.at[k],
            device_id={"ab": beside}, device_id_type=MESH,
        )

    def cross_next(chunk, k):
        for group in chunk:
            cross_copy(group, k).wait_send()
        later = k + AHEAD

        @pl.when(later < pieces)
        def _():
            for group in chunk:
                cross_copy(group, later).start()

        if chunk == chunks[0]:
            @pl.when(later >= pieces)
            def _():
                for group in chunks[1]:
                    cross_copy(group, later - pieces).start()

    @pl.loop(0, AHEAD)
    def _(k):
        for group in chunks[0]:
            cross_copy(group, k).start()

    @pl.loop(0, pieces)
    def _(k):
        near_copy(k).start()

    index_copies = [
        pltpu.make_async_copy(src, dst, index_sem.at[i])
        for i, (src, dst) in enumerate(
            ((c_hbm, c_ref), (d_hbm, d_ref), (qa_hbm, qa_ref), (qb_hbm, qb_ref)))
    ]
    for copy in index_copies:
        copy.start()
    for copy in index_copies:
        copy.wait()
    same = c_ref[...] == d_ref[...]
    weights[0:1, :] = jnp.where(same, F32(0.5), F32(1.0))
    weights[1:2, :] = jnp.where(same, F32(0.0), F32(1.0))

    def product(cols, *operands):
        x = jnp.concatenate([
            held[slot, slab, rows, cols] * weights[slab:slab + 1, cols]
            for slot, slab, rows in operands
        ], axis=0)
        high, low = split(x)
        count = x.shape[0]
        out = jnp.dot(jnp.concatenate([high, low], axis=0), v_split[cols, :],
                      preferred_element_type=F32)
        return out[:count, :q] + (out[count:, :q] + out[:count, q:])

    def send_sums(sums, at, row, slab, slabs, count):
        these = pl.ds(slab, slabs)

        @pl.loop(0, count, step=8)
        def _(done):
            values = [sums[pl.ds(pl.multiple_of(at + s * count + done, 8), 8), :]
                      for s in range(slabs)]
            for m in range(8 // unit):
                message = (row + done) // unit + m
                for s in range(slabs):
                    part[message, slab + s] = values[s][m * unit:(m + 1) * unit]
                owner = message // mine

                @pl.when(owner != me)
                def _():
                    slot = lax.rem(me - owner - 1 + n, n)
                    pltpu.make_async_remote_copy(
                        src_ref=part.at[message, these],
                        dst_ref=recv.at[slot, lax.rem(message, mine), these],
                        send_sem=rs, recv_sem=rr,
                        device_id={"cd": owner}, device_id_type=MESH,
                    ).start()

    own.wait()
    near[...] = jnp.zeros_like(near)

    @pl.loop(0, pieces)
    def _(k):
        cols = columns(k)
        v_copy(k).wait()
        v_split[cols, :q], v_split[cols, q:] = split(v[cols, :])
        near_copy(k).wait_recv()
        near[...] += product(
            cols, *((slot, slab, pl.ds(0, block)) for slot in (0, 1) for slab in range(2)))

        for early in range(EARLY):
            @pl.when(k == (early + 1) * pieces // EARLY - 1)
            def _():
                cross_next(chunks[0], early)

    for at, owner in ((0, j), (1, beside)):
        send_sums(near, at * 2 * block, owner * block, 0, 2, block)

    blocks = ((2, across, parity), (3, far, 1 - parity))

    def forward(chunk, k):
        for group in chunk:
            cross_copy(group, k).wait_recv()
            pass_copy(group, k).start()
        if chunk == chunks[0]:
            @pl.when(k >= EARLY)
            def _():
                cross_next(chunk, k)
        else:
            cross_next(chunk, k)

    def clear(chunk):
        size = sum(2 * groups[group][1] * groups[group][2] for group in chunk)
        total[:size, :] = jnp.zeros((size, q), F32)

    def add(chunk, k):
        for group in chunk:
            pass_copy(group, k).wait_recv()
        found = product(columns(k), *(
            (slot, slab + s, pl.ds(first_row(group, odd), count))
            for group in chunk for slab, slabs, count in (groups[group],)
            for slot, _, odd in blocks for s in range(slabs)))
        total[:found.shape[0], :] += found

    def finish(chunk):
        at = 0
        for group in chunk:
            slab, slabs, count = groups[group]
            for _, owner, odd in blocks:
                send_sums(total, at, owner * block + first_row(group, odd), slab, slabs, count)
                at += slabs * count

    clear(chunks[0])

    @pl.loop(0, pieces + LAG)
    def _(t):
        @pl.when(t < pieces)
        def _():
            forward(chunks[0], t)

        @pl.when(t >= pieces)
        def _():
            forward(chunks[1], t - pieces)

        @pl.when(t >= LAG)
        def _():
            add(chunks[0], t - LAG)

    finish(chunks[0])
    clear(chunks[1])

    @pl.loop(LAG, pieces + LAG)
    def _(t):
        @pl.when(t < pieces)
        def _():
            forward(chunks[1], t)

        add(chunks[1], t - LAG)

    finish(chunks[1])

    @pl.loop(0, pieces)
    def _(k):
        near_copy(k).wait_send()
        for group in range(len(groups)):
            pass_copy(group, k).wait_send()

    keep = jnp.where(qa_ref[...] == qb_ref[...], F32(0.0), F32(0.5)).reshape(1, q)
    pltpu.make_async_copy(recv, recv, rr).wait()
    for m in range(mine):
        sums = part[me * mine + m]
        sums = lax.fori_loop(0, n - 1, lambda k, acc: acc + recv[k, m], sums)
        out_ref[0, m * unit:(m + 1) * unit, :] = sums[0] * F32(0.5)
        out_ref[1, m * unit:(m + 1) * unit, :] = sums[1] * keep

    pltpu.make_async_copy(recv, recv, rs).wait()


def local(n, amplitudes, integrals, c_index, d_index, a_index, b_index):
    _, block, depth = amplitudes.shape
    q = integrals.shape[1]
    rows = 4 * block // n
    unit = min(8, rows)
    pieces = depth // DEPTH
    dma = pltpu.SemaphoreType.DMA
    out = pl.pallas_call(
        functools.partial(kernel, n),
        out_shape=jax.ShapeDtypeStruct((2, rows, q), F32),
        in_specs=[pl.BlockSpec(memory_space=pltpu.HBM)] * 6,
        out_specs=pl.BlockSpec(memory_space=pltpu.VMEM),
        scratch_shapes=[
            pltpu.VMEM((4, 2, block, depth), F32),
            pltpu.VMEM((depth, q), F32),
            pltpu.VMEM((depth, 2 * q), BF16),
            pltpu.VMEM((2, depth), F32),
            pltpu.VMEM((1, depth), jnp.int32),
            pltpu.VMEM((1, depth), jnp.int32),
            pltpu.VMEM((q,), jnp.int32),
            pltpu.VMEM((q,), jnp.int32),
            pltpu.VMEM((4 * block, q), F32),
            pltpu.VMEM((4 * block, q), F32),
            pltpu.VMEM((4 * block // unit, 2, unit, q), F32),
            pltpu.VMEM((n - 1, rows // unit, 2, unit, q), F32),
            dma, dma((pieces,)), dma((4,)), dma((pieces,)), dma((pieces,)),
            dma((2, pieces)), dma((2, pieces)), dma((2, pieces)), dma((2, pieces)), dma, dma,
        ],
        compiler_params=pltpu.CompilerParams(
            collective_id=0, has_side_effects=True, vmem_limit_bytes=44 * 1024 * 1024
        ),
        cost_estimate=pl.CostEstimate(
            flops=3 * 2 * 8 * block * depth * q,
            bytes_accessed=4 * depth * (q + 2 * block), transcendentals=0,
        ),
    )(*(pltpu.with_memory_space_constraint(x, pltpu.HBM) for x in (
        amplitudes, integrals, c_index.reshape(1, -1), d_index.reshape(1, -1), a_index, b_index)))
    return jnp.transpose(out, (1, 0, 2))


def solution(mesh):
    placed = (P(None, "ab", "cd"), P("cd", "ab"), P("cd"), P("cd"), P("ab"), P("ab"))
    return jax.shard_map(
        functools.partial(local, mesh.shape["cd"]), mesh=mesh, in_specs=placed,
        out_specs=P("cd", None, "ab"), check_vma=False,
    )
```

```python
import functools

import jax
import jax.numpy as jnp
from jax import lax
from jax.experimental import pallas as pl
from jax.experimental.pallas import tpu as pltpu
from jax.sharding import PartitionSpec as P

MESH = pl.DeviceIdType.MESH
BF16 = jnp.bfloat16
F32 = jnp.float32

LAST = 8
DEPTH = 1792
LAG = 1


def split(x):
    high = x.astype(BF16)
    return high, (x - high.astype(F32)).astype(BF16)


def kernel(n, a_hbm, v_hbm, c_hbm, d_hbm, qa_hbm, qb_hbm, out_ref,
           held, v, v_split, weights, c_ref, d_ref, qa_ref, qb_ref, total, near, part, recv,
           own_sem, v_sem, index_sem, cs, cr, xs, xr, fs, fr, rs, rr):
    me = lax.axis_index("cd")
    j = lax.axis_index("ab")
    beside = j + 1 - 2 * lax.rem(j, 2)
    across = lax.rem(j + 2, 4)
    far = lax.rem(beside + 2, 4)
    block = a_hbm.shape[1]
    depth = a_hbm.shape[2]
    pieces = depth // DEPTH
    q = out_ref.shape[2]
    groups = ((0, 2, block - LAST), (0, 2, LAST))
    chunks = ((0,), (1,))

    def first_row(group, parity):
        row = LAST * (1 - parity) if group == 0 else (block - LAST) * parity
        return pl.multiple_of(row, 8)

    unit = part.shape[2]
    mine = recv.shape[1]

    barrier = pltpu.get_barrier_semaphore()
    for other in (beside, across):
        pl.semaphore_signal(barrier, inc=1, device_id={"ab": other}, device_id_type=MESH)

    @pl.loop(1, n)
    def _(step):
        pl.semaphore_signal(
            barrier, inc=1, device_id={"cd": lax.rem(me + step, n)}, device_id_type=MESH
        )

    own = pltpu.make_async_copy(a_hbm, held.at[0], own_sem)
    own.start()

    def v_copy(k):
        at = pl.ds(pl.multiple_of(k * DEPTH, DEPTH), DEPTH)
        return pltpu.make_async_copy(v_hbm.at[at], v.at[at], v_sem.at[k])

    @pl.loop(0, pieces)
    def _(k):
        v_copy(k).start()

    pl.semaphore_wait(barrier, n + 1)

    def columns(k):
        return pl.ds(pl.multiple_of(k * DEPTH, DEPTH), DEPTH)

    parity = lax.rem(j, 2)

    def window(group, k):
        slab, slabs, count = groups[group]
        return pl.ds(slab, slabs), pl.ds(first_row(group, parity), count), columns(k)

    def cross_copy(group, k):
        at = window(group, k)
        return pltpu.make_async_remote_copy(
            src_ref=a_hbm.at[*at], dst_ref=held.at[2, *at],
            send_sem=xs.at[group, k], recv_sem=xr.at[group, k],
            device_id={"ab": across}, device_id_type=MESH,
        )

    def pass_copy(group, k):
        at = window(group, k)
        return pltpu.make_async_remote_copy(
            src_ref=held.at[2, *at], dst_ref=held.at[3, *at],
            send_sem=fs.at[group, k], recv_sem=fr.at[group, k],
            device_id={"ab": beside}, device_id_type=MESH,
        )

    def near_copy(k):
        cols = columns(k)
        return pltpu.make_async_remote_copy(
            src_ref=a_hbm.at[:, :, cols], dst_ref=held.at[1, :, :, cols],
            send_sem=cs.at[k], recv_sem=cr.at[k],
            device_id={"ab": beside}, device_id_type=MESH,
        )

    @pl.loop(0, pieces)
    def _(k):
        for group in chunks[0]:
            cross_copy(group, k).start()

    @pl.loop(0, pieces)
    def _(k):
        near_copy(k).start()

    index_copies = [
        pltpu.make_async_copy(src, dst, index_sem.at[i])
        for i, (src, dst) in enumerate(
            ((c_hbm, c_ref), (d_hbm, d_ref), (qa_hbm, qa_ref), (qb_hbm, qb_ref)))
    ]
    for copy in index_copies:
        copy.start()
    for copy in index_copies:
        copy.wait()
    same = c_ref[...] == d_ref[...]
    weights[0:1, :] = jnp.where(same, F32(0.5), F32(1.0))
    weights[1:2, :] = jnp.where(same, F32(0.0), F32(1.0))

    def product(cols, *operands):
        x = jnp.concatenate([
            held[slot, slab, rows, cols] * weights[slab:slab + 1, cols]
            for slot, slab, rows in operands
        ], axis=0)
        high, low = split(x)
        count = x.shape[0]
        out = jnp.dot(jnp.concatenate([high, low], axis=0), v_split[cols, :],
                      preferred_element_type=F32)
        return out[:count, :q] + (out[count:, :q] + out[:count, q:])

    def send_sums(sums, at, row, slab, slabs, count):
        these = pl.ds(slab, slabs)

        @pl.loop(0, count, step=8)
        def _(done):
            values = [sums[pl.ds(pl.multiple_of(at + s * count + done, 8), 8), :]
                      for s in range(slabs)]
            for m in range(8 // unit):
                message = (row + done) // unit + m
                for s in range(slabs):
                    part[message, slab + s] = values[s][m * unit:(m + 1) * unit]
                owner = message // mine

                @pl.when(owner != me)
                def _():
                    slot = lax.rem(me - owner - 1 + n, n)
                    pltpu.make_async_remote_copy(
                        src_ref=part.at[message, these],
                        dst_ref=recv.at[slot, lax.rem(message, mine), these],
                        send_sem=rs, recv_sem=rr,
                        device_id={"cd": owner}, device_id_type=MESH,
                    ).start()

    own.wait()
    near[...] = jnp.zeros_like(near)

    @pl.loop(0, pieces)
    def _(k):
        cols = columns(k)
        v_copy(k).wait()
        v_split[cols, :q], v_split[cols, q:] = split(v[cols, :])
        near_copy(k).wait_recv()
        near[...] += product(
            cols, *((slot, slab, pl.ds(0, block)) for slot in (0, 1) for slab in range(2)))

    for at, owner in ((0, j), (1, beside)):
        send_sums(near, at * 2 * block, owner * block, 0, 2, block)

    blocks = ((2, across, parity), (3, far, 1 - parity))

    def forward(chunk, k):
        for group in chunk:
            cross_copy(group, k).wait_recv()
            pass_copy(group, k).start()
        if chunk == chunks[0]:
            for group in chunk:
                cross_copy(group, k).wait_send()
            for group in chunks[1]:
                cross_copy(group, k).start()

    def clear(chunk):
        size = sum(2 * groups[group][1] * groups[group][2] for group in chunk)
        total[:size, :] = jnp.zeros((size, q), F32)

    def add(chunk, k):
        for group in chunk:
            pass_copy(group, k).wait_recv()
        found = product(columns(k), *(
            (slot, slab + s, pl.ds(first_row(group, odd), count))
            for group in chunk for slab, slabs, count in (groups[group],)
            for slot, _, odd in blocks for s in range(slabs)))
        total[:found.shape[0], :] += found

    def finish(chunk):
        at = 0
        for group in chunk:
            slab, slabs, count = groups[group]
            for _, owner, odd in blocks:
                send_sums(total, at, owner * block + first_row(group, odd), slab, slabs, count)
                at += slabs * count

    clear(chunks[0])

    @pl.loop(0, pieces + LAG)
    def _(t):
        @pl.when(t < pieces)
        def _():
            forward(chunks[0], t)

        @pl.when(t >= pieces)
        def _():
            forward(chunks[1], t - pieces)

        @pl.when(t >= LAG)
        def _():
            add(chunks[0], t - LAG)

    finish(chunks[0])
    clear(chunks[1])

    @pl.loop(LAG, pieces + LAG)
    def _(t):
        @pl.when(t < pieces)
        def _():
            forward(chunks[1], t)

        add(chunks[1], t - LAG)

    finish(chunks[1])

    @pl.loop(0, pieces)
    def _(k):
        near_copy(k).wait_send()
        for group in range(len(groups)):
            pass_copy(group, k).wait_send()
        for group in chunks[1]:
            cross_copy(group, k).wait_send()

    keep = jnp.where(qa_ref[...] == qb_ref[...], F32(0.0), F32(0.5)).reshape(1, q)
    pltpu.make_async_copy(recv, recv, rr).wait()
    for m in range(mine):
        sums = part[me * mine + m]
        sums = lax.fori_loop(0, n - 1, lambda k, acc: acc + recv[k, m], sums)
        out_ref[0, m * unit:(m + 1) * unit, :] = sums[0] * F32(0.5)
        out_ref[1, m * unit:(m + 1) * unit, :] = sums[1] * keep

    pltpu.make_async_copy(recv, recv, rs).wait()


def local(n, amplitudes, integrals, c_index, d_index, a_index, b_index):
    _, block, depth = amplitudes.shape
    q = integrals.shape[1]
    rows = 4 * block // n
    unit = min(8, rows)
    pieces = depth // DEPTH
    dma = pltpu.SemaphoreType.DMA
    out = pl.pallas_call(
        functools.partial(kernel, n),
        out_shape=jax.ShapeDtypeStruct((2, rows, q), F32),
        in_specs=[pl.BlockSpec(memory_space=pltpu.HBM)] * 6,
        out_specs=pl.BlockSpec(memory_space=pltpu.VMEM),
        scratch_shapes=[
            pltpu.VMEM((4, 2, block, depth), F32),
            pltpu.VMEM((depth, q), F32),
            pltpu.VMEM((depth, 2 * q), BF16),
            pltpu.VMEM((2, depth), F32),
            pltpu.VMEM((1, depth), jnp.int32),
            pltpu.VMEM((1, depth), jnp.int32),
            pltpu.VMEM((q,), jnp.int32),
            pltpu.VMEM((q,), jnp.int32),
            pltpu.VMEM((4 * block, q), F32),
            pltpu.VMEM((4 * block, q), F32),
            pltpu.VMEM((4 * block // unit, 2, unit, q), F32),
            pltpu.VMEM((n - 1, rows // unit, 2, unit, q), F32),
            dma, dma((pieces,)), dma((4,)), dma((pieces,)), dma((pieces,)),
            dma((2, pieces)), dma((2, pieces)), dma((2, pieces)), dma((2, pieces)), dma, dma,
        ],
        compiler_params=pltpu.CompilerParams(
            collective_id=0, has_side_effects=True, vmem_limit_bytes=44 * 1024 * 1024
        ),
        cost_estimate=pl.CostEstimate(
            flops=3 * 2 * 8 * block * depth * q,
            bytes_accessed=4 * depth * (q + 2 * block), transcendentals=0,
        ),
    )(*(pltpu.with_memory_space_constraint(x, pltpu.HBM) for x in (
        amplitudes, integrals, c_index.reshape(1, -1), d_index.reshape(1, -1), a_index, b_index)))
    return jnp.transpose(out, (1, 0, 2))


def solution(mesh):
    placed = (P(None, "ab", "cd"), P("cd", "ab"), P("cd"), P("cd"), P("ab"), P("ab"))
    return jax.shard_map(
        functools.partial(local, mesh.shape["cd"]), mesh=mesh, in_specs=placed,
        out_specs=P("cd", None, "ab"), check_vma=False,
    )
```

```python
import functools

import jax
import jax.numpy as jnp
from jax import lax
from jax.experimental import pallas as pl
from jax.experimental.pallas import tpu as pltpu
from jax.sharding import PartitionSpec as P

MESH = pl.DeviceIdType.MESH
BF16 = jnp.bfloat16
F32 = jnp.float32

LAST = 8
DEPTH = 1024
LAG = 1


def split(x):
    high = x.astype(BF16)
    return high, (x - high.astype(F32)).astype(BF16)


def kernel(n, a_hbm, v_hbm, c_hbm, d_hbm, qa_hbm, qb_hbm, out_ref,
           held, v, v_split, weights, c_ref, d_ref, qa_ref, qb_ref, total, near, part, recv,
           own_sem, v_sem, index_sem, cs, cr, xs, xr, fs, fr, rs, rr, go_sem, met_sem):
    me = lax.axis_index("cd")
    j = lax.axis_index("ab")
    beside = j + 1 - 2 * lax.rem(j, 2)
    across = lax.rem(j + 2, 4)
    far = lax.rem(beside + 2, 4)
    block = a_hbm.shape[1]
    depth = a_hbm.shape[2]
    pieces = depth // DEPTH
    q = out_ref.shape[2]
    groups = ((0, 2, block - LAST), (0, 2, LAST))
    chunks = ((0,), (1,))

    def first_row(group, parity):
        row = LAST * (1 - parity) if group == 0 else (block - LAST) * parity
        return pl.multiple_of(row, 8)

    unit = part.shape[2]
    mine = recv.shape[1]

    first_half = j < 2
    second_half = j >= 2
    barrier = pltpu.get_barrier_semaphore()
    pl.semaphore_signal(barrier, inc=1, device_id={"ab": beside}, device_id_type=MESH)

    @pl.when(second_half)
    def _():
        pl.semaphore_signal(barrier, inc=1, device_id={"ab": across}, device_id_type=MESH)

    own = pltpu.make_async_copy(a_hbm, held.at[0], own_sem)
    own.start()

    def v_copy(k):
        at = pl.ds(pl.multiple_of(k * DEPTH, DEPTH), DEPTH)
        return pltpu.make_async_copy(v_hbm.at[at], v.at[at], v_sem.at[k])

    @pl.loop(0, pieces)
    def _(k):
        v_copy(k).start()

    @pl.when(first_half)
    def _():
        pl.semaphore_wait(barrier, 2)
        pl.semaphore_signal(go_sem, inc=1, device_id={"ab": across}, device_id_type=MESH)

    @pl.when(second_half)
    def _():
        pl.semaphore_wait(go_sem, 1)

    def columns(k):
        return pl.ds(pl.multiple_of(k * DEPTH, DEPTH), DEPTH)

    parity = lax.rem(j, 2)

    def window(group, k):
        slab, slabs, count = groups[group]
        return pl.ds(slab, slabs), pl.ds(first_row(group, parity), count), columns(k)

    def cross_copy(group, k):
        at = window(group, k)
        return pltpu.make_async_remote_copy(
            src_ref=a_hbm.at[*at], dst_ref=held.at[2, *at],
            send_sem=xs.at[group, k], recv_sem=xr.at[group, k],
            device_id={"ab": across}, device_id_type=MESH,
        )

    def pass_copy(group, k):
        at = window(group, k)
        return pltpu.make_async_remote_copy(
            src_ref=held.at[2, *at], dst_ref=held.at[3, *at],
            send_sem=fs.at[group, k], recv_sem=fr.at[group, k],
            device_id={"ab": beside}, device_id_type=MESH,
        )

    def near_copy(k):
        cols = columns(k)
        return pltpu.make_async_remote_copy(
            src_ref=a_hbm.at[:, :, cols], dst_ref=held.at[1, :, :, cols],
            send_sem=cs.at[k], recv_sem=cr.at[k],
            device_id={"ab": beside}, device_id_type=MESH,
        )

    @pl.loop(0, pieces)
    def _(k):
        for group in chunks[0]:
            cross_copy(group, k).start()

    @pl.when(second_half)
    def _():
        @pl.loop(1, n)
        def _(step):
            pl.semaphore_signal(
                barrier, inc=1, device_id={"cd": lax.rem(me + step, n)}, device_id_type=MESH
            )

        pl.semaphore_wait(barrier, n)
        pl.semaphore_signal(met_sem, inc=1, device_id={"ab": across}, device_id_type=MESH)

    @pl.loop(0, pieces)
    def _(k):
        near_copy(k).start()

    index_copies = [
        pltpu.make_async_copy(src, dst, index_sem.at[i])
        for i, (src, dst) in enumerate(
            ((c_hbm, c_ref), (d_hbm, d_ref), (qa_hbm, qa_ref), (qb_hbm, qb_ref)))
    ]
    for copy in index_copies:
        copy.start()
    for copy in index_copies:
        copy.wait()
    same = c_ref[...] == d_ref[...]
    weights[0:1, :] = jnp.where(same, F32(0.5), F32(1.0))
    weights[1:2, :] = jnp.where(same, F32(0.0), F32(1.0))

    def product(cols, *operands):
        x = jnp.concatenate([
            held[slot, slab, rows, cols] * weights[slab:slab + 1, cols]
            for slot, slab, rows in operands
        ], axis=0)
        high, low = split(x)
        count = x.shape[0]
        out = jnp.dot(jnp.concatenate([high, low], axis=0), v_split[cols, :],
                      preferred_element_type=F32)
        return out[:count, :q] + (out[count:, :q] + out[:count, q:])

    def send_sums(sums, at, row, slab, slabs, count):
        these = pl.ds(slab, slabs)

        @pl.loop(0, count, step=8)
        def _(done):
            values = [sums[pl.ds(pl.multiple_of(at + s * count + done, 8), 8), :]
                      for s in range(slabs)]
            for m in range(8 // unit):
                message = (row + done) // unit + m
                for s in range(slabs):
                    part[message, slab + s] = values[s][m * unit:(m + 1) * unit]
                owner = message // mine

                @pl.when(owner != me)
                def _():
                    slot = lax.rem(me - owner - 1 + n, n)
                    pltpu.make_async_remote_copy(
                        src_ref=part.at[message, these],
                        dst_ref=recv.at[slot, lax.rem(message, mine), these],
                        send_sem=rs, recv_sem=rr,
                        device_id={"cd": owner}, device_id_type=MESH,
                    ).start()

    own.wait()
    near[...] = jnp.zeros_like(near)

    @pl.loop(0, pieces)
    def _(k):
        cols = columns(k)
        v_copy(k).wait()
        v_split[cols, :q], v_split[cols, q:] = split(v[cols, :])
        near_copy(k).wait_recv()
        near[...] += product(
            cols, *((slot, slab, pl.ds(0, block)) for slot in (0, 1) for slab in range(2)))

    @pl.when(first_half)
    def _():
        pl.semaphore_wait(met_sem, 1)

    for at, owner in ((0, j), (1, beside)):
        send_sums(near, at * 2 * block, owner * block, 0, 2, block)

    blocks = ((2, across, parity), (3, far, 1 - parity))

    def forward(chunk, k):
        for group in chunk:
            cross_copy(group, k).wait_recv()
            pass_copy(group, k).start()
        if chunk == chunks[0]:
            for group in chunk:
                cross_copy(group, k).wait_send()
            for group in chunks[1]:
                cross_copy(group, k).start()

    def clear(chunk):
        size = sum(2 * groups[group][1] * groups[group][2] for group in chunk)
        total[:size, :] = jnp.zeros((size, q), F32)

    def add(chunk, k):
        for group in chunk:
            pass_copy(group, k).wait_recv()
        found = product(columns(k), *(
            (slot, slab + s, pl.ds(first_row(group, odd), count))
            for group in chunk for slab, slabs, count in (groups[group],)
            for slot, _, odd in blocks for s in range(slabs)))
        total[:found.shape[0], :] += found

    def finish(chunk):
        at = 0
        for group in chunk:
            slab, slabs, count = groups[group]
            for _, owner, odd in blocks:
                send_sums(total, at, owner * block + first_row(group, odd), slab, slabs, count)
                at += slabs * count

    clear(chunks[0])

    @pl.loop(0, pieces + LAG)
    def _(t):
        @pl.when(t < pieces)
        def _():
            forward(chunks[0], t)

        @pl.when(t >= pieces)
        def _():
            forward(chunks[1], t - pieces)

        @pl.when(t >= LAG)
        def _():
            add(chunks[0], t - LAG)

    finish(chunks[0])
    clear(chunks[1])

    @pl.loop(LAG, pieces + LAG)
    def _(t):
        @pl.when(t < pieces)
        def _():
            forward(chunks[1], t)

        add(chunks[1], t - LAG)

    finish(chunks[1])

    @pl.loop(0, pieces)
    def _(k):
        near_copy(k).wait_send()
        for group in range(len(groups)):
            pass_copy(group, k).wait_send()
        for group in chunks[1]:
            cross_copy(group, k).wait_send()

    keep = jnp.where(qa_ref[...] == qb_ref[...], F32(0.0), F32(0.5)).reshape(1, q)
    pltpu.make_async_copy(recv, recv, rr).wait()
    for m in range(mine):
        sums = part[me * mine + m]
        sums = lax.fori_loop(0, n - 1, lambda k, acc: acc + recv[k, m], sums)
        out_ref[0, m * unit:(m + 1) * unit, :] = sums[0] * F32(0.5)
        out_ref[1, m * unit:(m + 1) * unit, :] = sums[1] * keep

    pltpu.make_async_copy(recv, recv, rs).wait()


def local(n, amplitudes, integrals, c_index, d_index, a_index, b_index):
    _, block, depth = amplitudes.shape
    q = integrals.shape[1]
    rows = 4 * block // n
    unit = min(8, rows)
    pieces = depth // DEPTH
    dma = pltpu.SemaphoreType.DMA
    out = pl.pallas_call(
        functools.partial(kernel, n),
        out_shape=jax.ShapeDtypeStruct((2, rows, q), F32),
        in_specs=[pl.BlockSpec(memory_space=pltpu.HBM)] * 6,
        out_specs=pl.BlockSpec(memory_space=pltpu.VMEM),
        scratch_shapes=[
            pltpu.VMEM((4, 2, block, depth), F32),
            pltpu.VMEM((depth, q), F32),
            pltpu.VMEM((depth, 2 * q), BF16),
            pltpu.VMEM((2, depth), F32),
            pltpu.VMEM((1, depth), jnp.int32),
            pltpu.VMEM((1, depth), jnp.int32),
            pltpu.VMEM((q,), jnp.int32),
            pltpu.VMEM((q,), jnp.int32),
            pltpu.VMEM((4 * block, q), F32),
            pltpu.VMEM((4 * block, q), F32),
            pltpu.VMEM((4 * block // unit, 2, unit, q), F32),
            pltpu.VMEM((n - 1, rows // unit, 2, unit, q), F32),
            dma, dma((pieces,)), dma((4,)), dma((pieces,)), dma((pieces,)),
            dma((2, pieces)), dma((2, pieces)), dma((2, pieces)), dma((2, pieces)), dma, dma,
            pltpu.SemaphoreType.REGULAR, pltpu.SemaphoreType.REGULAR,
        ],
        compiler_params=pltpu.CompilerParams(
            collective_id=0, has_side_effects=True, vmem_limit_bytes=44 * 1024 * 1024
        ),
        cost_estimate=pl.CostEstimate(
            flops=3 * 2 * 8 * block * depth * q,
            bytes_accessed=4 * depth * (q + 2 * block), transcendentals=0,
        ),
    )(*(pltpu.with_memory_space_constraint(x, pltpu.HBM) for x in (
        amplitudes, integrals, c_index.reshape(1, -1), d_index.reshape(1, -1), a_index, b_index)))
    return jnp.transpose(out, (1, 0, 2))


def solution(mesh):
    placed = (P(None, "ab", "cd"), P("cd", "ab"), P("cd"), P("cd"), P("ab"), P("ab"))
    return jax.shard_map(
        functools.partial(local, mesh.shape["cd"]), mesh=mesh, in_specs=placed,
        out_specs=P("cd", None, "ab"), check_vma=False,
    )
```

```python
import functools

import jax
import jax.numpy as jnp
from jax import lax
from jax.experimental import pallas as pl
from jax.experimental.pallas import tpu as pltpu
from jax.sharding import PartitionSpec as P

MESH = pl.DeviceIdType.MESH
BF16 = jnp.bfloat16
F32 = jnp.float32

LAST = 8
DEPTH = 1792
SHORT = 768


def split(x):
    high = x.astype(BF16)
    return high, (x - high.astype(F32)).astype(BF16)


def kernel(n, a_hbm, v_hbm, c_hbm, d_hbm, qa_hbm, qb_hbm, out_ref,
           held, v, v_split, weights, c_ref, d_ref, qa_ref, qb_ref, total, near, part, recv,
           own_sem, v_sem, index_sem, cs, cr, xs, xr, fs, fr, rs, rr, go_sem, met_sem):
    me = lax.axis_index("cd")
    j = lax.axis_index("ab")
    beside = j + 1 - 2 * lax.rem(j, 2)
    across = lax.rem(j + 2, 4)
    far = lax.rem(beside + 2, 4)
    block = a_hbm.shape[1]
    depth = a_hbm.shape[2]
    pieces = depth // DEPTH
    q = out_ref.shape[2]
    groups = ((0, 2, block - LAST), (0, 2, LAST))
    chunks = ((0,), (1,))

    def first_row(group, parity):
        row = LAST * (1 - parity) if group == 0 else (block - LAST) * parity
        return pl.multiple_of(row, 8)

    unit = part.shape[2]
    mine = recv.shape[1]

    first_half = j < 2
    second_half = j >= 2
    barrier = pltpu.get_barrier_semaphore()
    pl.semaphore_signal(barrier, inc=1, device_id={"ab": beside}, device_id_type=MESH)

    @pl.when(second_half)
    def _():
        pl.semaphore_signal(barrier, inc=1, device_id={"ab": across}, device_id_type=MESH)

    own = pltpu.make_async_copy(a_hbm, held.at[0], own_sem)
    own.start()

    def v_copy(k):
        at = pl.ds(pl.multiple_of(k * DEPTH, DEPTH), DEPTH)
        return pltpu.make_async_copy(v_hbm.at[at], v.at[at], v_sem.at[k])

    @pl.loop(0, pieces)
    def _(k):
        v_copy(k).start()

    @pl.when(first_half)
    def _():
        pl.semaphore_wait(barrier, 2)
        pl.semaphore_signal(go_sem, inc=1, device_id={"ab": across}, device_id_type=MESH)

    @pl.when(second_half)
    def _():
        pl.semaphore_wait(go_sem, 1)

    def columns(k):
        return pl.ds(pl.multiple_of(k * DEPTH, DEPTH), DEPTH)

    parity = lax.rem(j, 2)

    def span(group, k):
        if group == 1 and isinstance(k, int) and k >= pieces - 1:
            if k == pieces - 1:
                return pl.ds(depth - DEPTH, DEPTH - SHORT)
            return pl.ds(depth - SHORT, SHORT)
        return columns(k)

    def window(group, k):
        slab, slabs, count = groups[group]
        return pl.ds(slab, slabs), pl.ds(first_row(group, parity), count), span(group, k)

    def cross_copy(group, k):
        at = window(group, k)
        return pltpu.make_async_remote_copy(
            src_ref=a_hbm.at[*at], dst_ref=held.at[2, *at],
            send_sem=xs.at[group, k], recv_sem=xr.at[group, k],
            device_id={"ab": across}, device_id_type=MESH,
        )

    def pass_copy(group, k):
        at = window(group, k)
        return pltpu.make_async_remote_copy(
            src_ref=held.at[2, *at], dst_ref=held.at[3, *at],
            send_sem=fs.at[group, k], recv_sem=fr.at[group, k],
            device_id={"ab": beside}, device_id_type=MESH,
        )

    def near_copy(k):
        cols = columns(k)
        return pltpu.make_async_remote_copy(
            src_ref=a_hbm.at[:, :, cols], dst_ref=held.at[1, :, :, cols],
            send_sem=cs.at[k], recv_sem=cr.at[k],
            device_id={"ab": beside}, device_id_type=MESH,
        )

    @pl.loop(0, pieces)
    def _(k):
        for group in chunks[0]:
            cross_copy(group, k).start()

    @pl.when(second_half)
    def _():
        @pl.loop(1, n)
        def _(step):
            pl.semaphore_signal(
                barrier, inc=1, device_id={"cd": lax.rem(me + step, n)}, device_id_type=MESH
            )

        pl.semaphore_wait(barrier, n)
        pl.semaphore_signal(met_sem, inc=1, device_id={"ab": across}, device_id_type=MESH)

    @pl.loop(0, pieces)
    def _(k):
        near_copy(k).start()

    index_copies = [
        pltpu.make_async_copy(src, dst, index_sem.at[i])
        for i, (src, dst) in enumerate(
            ((c_hbm, c_ref), (d_hbm, d_ref), (qa_hbm, qa_ref), (qb_hbm, qb_ref)))
    ]
    for copy in index_copies:
        copy.start()
    for copy in index_copies:
        copy.wait()
    same = c_ref[...] == d_ref[...]
    weights[0:1, :] = jnp.where(same, F32(0.5), F32(1.0))
    weights[1:2, :] = jnp.where(same, F32(0.0), F32(1.0))

    def product(cols, *operands):
        x = jnp.concatenate([
            held[slot, slab, rows, cols] * weights[slab:slab + 1, cols]
            for slot, slab, rows in operands
        ], axis=0)
        high, low = split(x)
        count = x.shape[0]
        out = jnp.dot(jnp.concatenate([high, low], axis=0), v_split[cols, :],
                      preferred_element_type=F32)
        return out[:count, :q] + (out[count:, :q] + out[:count, q:])

    def send_sums(sums, at, row, slab, slabs, count):
        these = pl.ds(slab, slabs)

        @pl.loop(0, count, step=8)
        def _(done):
            values = [sums[pl.ds(pl.multiple_of(at + s * count + done, 8), 8), :]
                      for s in range(slabs)]
            for m in range(8 // unit):
                message = (row + done) // unit + m
                for s in range(slabs):
                    part[message, slab + s] = values[s][m * unit:(m + 1) * unit]
                owner = message // mine

                @pl.when(owner != me)
                def _():
                    slot = lax.rem(me - owner - 1 + n, n)
                    pltpu.make_async_remote_copy(
                        src_ref=part.at[message, these],
                        dst_ref=recv.at[slot, lax.rem(message, mine), these],
                        send_sem=rs, recv_sem=rr,
                        device_id={"cd": owner}, device_id_type=MESH,
                    ).start()

    own.wait()
    near[...] = jnp.zeros_like(near)

    @pl.loop(0, pieces)
    def _(k):
        cols = columns(k)
        v_copy(k).wait()
        v_split[cols, :q], v_split[cols, q:] = split(v[cols, :])
        near_copy(k).wait_recv()
        near[...] += product(
            cols, *((slot, slab, pl.ds(0, block)) for slot in (0, 1) for slab in range(2)))

    @pl.when(first_half)
    def _():
        pl.semaphore_wait(met_sem, 1)

    for at, owner in ((0, j), (1, beside)):
        send_sums(near, at * 2 * block, owner * block, 0, 2, block)

    blocks = ((2, across, parity), (3, far, 1 - parity))

    def forward(chunk, k):
        for group in chunk:
            cross_copy(group, k).wait_recv()
            pass_copy(group, k).start()
        if chunk == chunks[0]:
            for group in chunk:
                cross_copy(group, k).wait_send()

            @pl.when(k < pieces - 1)
            def _():
                cross_copy(1, k).start()

            @pl.when(k == pieces - 1)
            def _():
                cross_copy(1, pieces - 1).start()
                cross_copy(1, pieces).start()

    def clear(chunk):
        size = sum(2 * groups[group][1] * groups[group][2] for group in chunk)
        total[:size, :] = jnp.zeros((size, q), F32)

    def add(chunk, k):
        for group in chunk:
            pass_copy(group, k).wait_recv()
        found = product(span(chunk[0], k), *(
            (slot, slab + s, pl.ds(first_row(group, odd), count))
            for group in chunk for slab, slabs, count in (groups[group],)
            for slot, _, odd in blocks for s in range(slabs)))
        total[:found.shape[0], :] += found

    def finish(chunk):
        at = 0
        for group in chunk:
            slab, slabs, count = groups[group]
            for _, owner, odd in blocks:
                send_sums(total, at, owner * block + first_row(group, odd), slab, slabs, count)
                at += slabs * count

    clear(chunks[0])

    @pl.loop(0, pieces + 1)
    def _(t):
        @pl.when(t < pieces)
        def _():
            forward(chunks[0], t)

        @pl.when(t >= pieces)
        def _():
            forward(chunks[1], 0)

        @pl.when(t >= 1)
        def _():
            add(chunks[0], t - 1)

    finish(chunks[0])
    clear(chunks[1])

    for k in range(1, pieces + 2):
        if k <= pieces:
            forward(chunks[1], k)
        add(chunks[1], k - 1)

    finish(chunks[1])

    @pl.loop(0, pieces)
    def _(k):
        near_copy(k).wait_send()
        pass_copy(0, k).wait_send()

    for k in range(pieces + 1):
        pass_copy(1, k).wait_send()
        cross_copy(1, k).wait_send()

    keep = jnp.where(qa_ref[...] == qb_ref[...], F32(0.0), F32(0.5)).reshape(1, q)
    pltpu.make_async_copy(recv, recv, rr).wait()
    for m in range(mine):
        sums = part[me * mine + m]
        sums = lax.fori_loop(0, n - 1, lambda k, acc: acc + recv[k, m], sums)
        out_ref[0, m * unit:(m + 1) * unit, :] = sums[0] * F32(0.5)
        out_ref[1, m * unit:(m + 1) * unit, :] = sums[1] * keep

    pltpu.make_async_copy(recv, recv, rs).wait()


def local(n, amplitudes, integrals, c_index, d_index, a_index, b_index):
    _, block, depth = amplitudes.shape
    q = integrals.shape[1]
    rows = 4 * block // n
    unit = min(8, rows)
    pieces = depth // DEPTH
    dma = pltpu.SemaphoreType.DMA
    out = pl.pallas_call(
        functools.partial(kernel, n),
        out_shape=jax.ShapeDtypeStruct((2, rows, q), F32),
        in_specs=[pl.BlockSpec(memory_space=pltpu.HBM)] * 6,
        out_specs=pl.BlockSpec(memory_space=pltpu.VMEM),
        scratch_shapes=[
            pltpu.VMEM((4, 2, block, depth), F32),
            pltpu.VMEM((depth, q), F32),
            pltpu.VMEM((depth, 2 * q), BF16),
            pltpu.VMEM((2, depth), F32),
            pltpu.VMEM((1, depth), jnp.int32),
            pltpu.VMEM((1, depth), jnp.int32),
            pltpu.VMEM((q,), jnp.int32),
            pltpu.VMEM((q,), jnp.int32),
            pltpu.VMEM((4 * block, q), F32),
            pltpu.VMEM((4 * block, q), F32),
            pltpu.VMEM((4 * block // unit, 2, unit, q), F32),
            pltpu.VMEM((n - 1, rows // unit, 2, unit, q), F32),
            dma, dma((pieces,)), dma((4,)), dma((pieces,)), dma((pieces,)),
            dma((2, pieces + 1)), dma((2, pieces + 1)), dma((2, pieces + 1)), dma((2, pieces + 1)),
            dma, dma,
            pltpu.SemaphoreType.REGULAR, pltpu.SemaphoreType.REGULAR,
        ],
        compiler_params=pltpu.CompilerParams(
            collective_id=0, has_side_effects=True, vmem_limit_bytes=44 * 1024 * 1024
        ),
        cost_estimate=pl.CostEstimate(
            flops=3 * 2 * 8 * block * depth * q,
            bytes_accessed=4 * depth * (q + 2 * block), transcendentals=0,
        ),
    )(*(pltpu.with_memory_space_constraint(x, pltpu.HBM) for x in (
        amplitudes, integrals, c_index.reshape(1, -1), d_index.reshape(1, -1), a_index, b_index)))
    return jnp.transpose(out, (1, 0, 2))


def solution(mesh):
    placed = (P(None, "ab", "cd"), P("cd", "ab"), P("cd"), P("cd"), P("ab"), P("ab"))
    return jax.shard_map(
        functools.partial(local, mesh.shape["cd"]), mesh=mesh, in_specs=placed,
        out_specs=P("cd", None, "ab"), check_vma=False,
    )
```

```python
import functools

import jax
import jax.numpy as jnp
from jax import lax
from jax.experimental import pallas as pl
from jax.experimental.pallas import tpu as pltpu
from jax.sharding import PartitionSpec as P

MESH = pl.DeviceIdType.MESH
BF16 = jnp.bfloat16
F32 = jnp.float32

LAST = 8
DEPTH = 1024
LAG = 1


def split(x):
    high = x.astype(BF16)
    return high, (x - high.astype(F32)).astype(BF16)


def kernel(n, a_hbm, v_hbm, c_hbm, d_hbm, qa_hbm, qb_hbm, out_ref,
           held, v, v_split, weights, c_ref, d_ref, qa_ref, qb_ref, total, near, part, recv,
           own_sem, v_sem, index_sem, cs, cr, xs, xr, fs, fr, rs, rr, go_sem, met_sem):
    me = lax.axis_index("cd")
    j = lax.axis_index("ab")
    beside = j + 1 - 2 * lax.rem(j, 2)
    across = lax.rem(j + 2, 4)
    far = lax.rem(beside + 2, 4)
    block = a_hbm.shape[1]
    depth = a_hbm.shape[2]
    pieces = depth // DEPTH
    q = out_ref.shape[2]
    groups = ((0, 2, block - LAST), (0, 2, LAST))
    chunks = ((0,), (1,))

    def first_row(group, parity):
        row = LAST * (1 - parity) if group == 0 else (block - LAST) * parity
        return pl.multiple_of(row, 8)

    unit = part.shape[2]
    mine = recv.shape[1]

    first_half = j >= 2
    second_half = j < 2
    barrier = pltpu.get_barrier_semaphore()
    pl.semaphore_signal(barrier, inc=1, device_id={"ab": beside}, device_id_type=MESH)

    @pl.when(second_half)
    def _():
        pl.semaphore_signal(barrier, inc=1, device_id={"ab": across}, device_id_type=MESH)

    own = pltpu.make_async_copy(a_hbm, held.at[0], own_sem)
    own.start()

    def v_copy(k):
        at = pl.ds(pl.multiple_of(k * DEPTH, DEPTH), DEPTH)
        return pltpu.make_async_copy(v_hbm.at[at], v.at[at], v_sem.at[k])

    @pl.loop(0, pieces)
    def _(k):
        v_copy(k).start()

    @pl.when(first_half)
    def _():
        pl.semaphore_wait(barrier, 2)
        pl.semaphore_signal(go_sem, inc=1, device_id={"ab": across}, device_id_type=MESH)

    @pl.when(second_half)
    def _():
        pl.semaphore_wait(go_sem, 1)

    def columns(k):
        return pl.ds(pl.multiple_of(k * DEPTH, DEPTH), DEPTH)

    parity = lax.rem(j, 2)

    def window(group, k):
        slab, slabs, count = groups[group]
        return pl.ds(slab, slabs), pl.ds(first_row(group, parity), count), columns(k)

    def cross_copy(group, k):
        at = window(group, k)
        return pltpu.make_async_remote_copy(
            src_ref=a_hbm.at[*at], dst_ref=held.at[2, *at],
            send_sem=xs.at[group, k], recv_sem=xr.at[group, k],
            device_id={"ab": across}, device_id_type=MESH,
        )

    def pass_copy(group, k):
        at = window(group, k)
        return pltpu.make_async_remote_copy(
            src_ref=held.at[2, *at], dst_ref=held.at[3, *at],
            send_sem=fs.at[group, k], recv_sem=fr.at[group, k],
            device_id={"ab": beside}, device_id_type=MESH,
        )

    def near_copy(k):
        cols = columns(k)
        return pltpu.make_async_remote_copy(
            src_ref=a_hbm.at[:, :, cols], dst_ref=held.at[1, :, :, cols],
            send_sem=cs.at[k], recv_sem=cr.at[k],
            device_id={"ab": beside}, device_id_type=MESH,
        )

    @pl.loop(0, pieces)
    def _(k):
        for group in chunks[0]:
            cross_copy(group, k).start()

    @pl.when(second_half)
    def _():
        @pl.loop(1, n)
        def _(step):
            pl.semaphore_signal(
                barrier, inc=1, device_id={"cd": lax.rem(me + step, n)}, device_id_type=MESH
            )

        pl.semaphore_wait(barrier, n)
        pl.semaphore_signal(met_sem, inc=1, device_id={"ab": across}, device_id_type=MESH)

    @pl.loop(0, pieces)
    def _(k):
        near_copy(k).start()

    index_copies = [
        pltpu.make_async_copy(src, dst, index_sem.at[i])
        for i, (src, dst) in enumerate(
            ((c_hbm, c_ref), (d_hbm, d_ref), (qa_hbm, qa_ref), (qb_hbm, qb_ref)))
    ]
    for copy in index_copies:
        copy.start()
    for copy in index_copies:
        copy.wait()
    same = c_ref[...] == d_ref[...]
    weights[0:1, :] = jnp.where(same, F32(0.5), F32(1.0))
    weights[1:2, :] = jnp.where(same, F32(0.0), F32(1.0))

    def product(cols, *operands):
        x = jnp.concatenate([
            held[slot, slab, rows, cols] * weights[slab:slab + 1, cols]
            for slot, slab, rows in operands
        ], axis=0)
        high, low = split(x)
        count = x.shape[0]
        out = jnp.dot(jnp.concatenate([high, low], axis=0), v_split[cols, :],
                      preferred_element_type=F32)
        return out[:count, :q] + (out[count:, :q] + out[:count, q:])

    def send_sums(sums, at, row, slab, slabs, count):
        these = pl.ds(slab, slabs)

        @pl.loop(0, count, step=8)
        def _(done):
            values = [sums[pl.ds(pl.multiple_of(at + s * count + done, 8), 8), :]
                      for s in range(slabs)]
            for m in range(8 // unit):
                message = (row + done) // unit + m
                for s in range(slabs):
                    part[message, slab + s] = values[s][m * unit:(m + 1) * unit]
                owner = message // mine

                @pl.when(owner != me)
                def _():
                    slot = lax.rem(me - owner - 1 + n, n)
                    pltpu.make_async_remote_copy(
                        src_ref=part.at[message, these],
                        dst_ref=recv.at[slot, lax.rem(message, mine), these],
                        send_sem=rs, recv_sem=rr,
                        device_id={"cd": owner}, device_id_type=MESH,
                    ).start()

    own.wait()
    near[...] = jnp.zeros_like(near)

    @pl.loop(0, pieces)
    def _(k):
        cols = columns(k)
        v_copy(k).wait()
        v_split[cols, :q], v_split[cols, q:] = split(v[cols, :])
        near_copy(k).wait_recv()
        near[...] += product(
            cols, *((slot, slab, pl.ds(0, block)) for slot in (0, 1) for slab in range(2)))

    @pl.when(first_half)
    def _():
        pl.semaphore_wait(met_sem, 1)

    for at, owner in ((0, j), (1, beside)):
        send_sums(near, at * 2 * block, owner * block, 0, 2, block)

    blocks = ((2, across, parity), (3, far, 1 - parity))

    def forward(chunk, k):
        for group in chunk:
            cross_copy(group, k).wait_recv()
            pass_copy(group, k).start()
        if chunk == chunks[0]:
            for group in chunk:
                cross_copy(group, k).wait_send()
            for group in chunks[1]:
                cross_copy(group, k).start()

    def clear(chunk):
        size = sum(2 * groups[group][1] * groups[group][2] for group in chunk)
        total[:size, :] = jnp.zeros((size, q), F32)

    def add(chunk, k):
        for group in chunk:
            pass_copy(group, k).wait_recv()
        found = product(columns(k), *(
            (slot, slab + s, pl.ds(first_row(group, odd), count))
            for group in chunk for slab, slabs, count in (groups[group],)
            for slot, _, odd in blocks for s in range(slabs)))
        total[:found.shape[0], :] += found

    def finish(chunk):
        at = 0
        for group in chunk:
            slab, slabs, count = groups[group]
            for _, owner, odd in blocks:
                send_sums(total, at, owner * block + first_row(group, odd), slab, slabs, count)
                at += slabs * count

    clear(chunks[0])

    @pl.loop(0, pieces + LAG)
    def _(t):
        @pl.when(t < pieces)
        def _():
            forward(chunks[0], t)

        @pl.when(t >= pieces)
        def _():
            forward(chunks[1], t - pieces)

        @pl.when(t >= LAG)
        def _():
            add(chunks[0], t - LAG)

    finish(chunks[0])
    clear(chunks[1])

    @pl.loop(LAG, pieces + LAG)
    def _(t):
        @pl.when(t < pieces)
        def _():
            forward(chunks[1], t)

        add(chunks[1], t - LAG)

    finish(chunks[1])

    @pl.loop(0, pieces)
    def _(k):
        near_copy(k).wait_send()
        for group in range(len(groups)):
            pass_copy(group, k).wait_send()
        for group in chunks[1]:
            cross_copy(group, k).wait_send()

    keep = jnp.where(qa_ref[...] == qb_ref[...], F32(0.0), F32(0.5)).reshape(1, q)
    pltpu.make_async_copy(recv, recv, rr).wait()
    for m in range(mine):
        sums = part[me * mine + m]
        sums = lax.fori_loop(0, n - 1, lambda k, acc: acc + recv[k, m], sums)
        out_ref[0, m * unit:(m + 1) * unit, :] = sums[0] * F32(0.5)
        out_ref[1, m * unit:(m + 1) * unit, :] = sums[1] * keep

    pltpu.make_async_copy(recv, recv, rs).wait()


def local(n, amplitudes, integrals, c_index, d_index, a_index, b_index):
    _, block, depth = amplitudes.shape
    q = integrals.shape[1]
    rows = 4 * block // n
    unit = min(8, rows)
    pieces = depth // DEPTH
    dma = pltpu.SemaphoreType.DMA
    out = pl.pallas_call(
        functools.partial(kernel, n),
        out_shape=jax.ShapeDtypeStruct((2, rows, q), F32),
        in_specs=[pl.BlockSpec(memory_space=pltpu.HBM)] * 6,
        out_specs=pl.BlockSpec(memory_space=pltpu.VMEM),
        scratch_shapes=[
            pltpu.VMEM((4, 2, block, depth), F32),
            pltpu.VMEM((depth, q), F32),
            pltpu.VMEM((depth, 2 * q), BF16),
            pltpu.VMEM((2, depth), F32),
            pltpu.VMEM((1, depth), jnp.int32),
            pltpu.VMEM((1, depth), jnp.int32),
            pltpu.VMEM((q,), jnp.int32),
            pltpu.VMEM((q,), jnp.int32),
            pltpu.VMEM((4 * block, q), F32),
            pltpu.VMEM((4 * block, q), F32),
            pltpu.VMEM((4 * block // unit, 2, unit, q), F32),
            pltpu.VMEM((n - 1, rows // unit, 2, unit, q), F32),
            dma, dma((pieces,)), dma((4,)), dma((pieces,)), dma((pieces,)),
            dma((2, pieces)), dma((2, pieces)), dma((2, pieces)), dma((2, pieces)), dma, dma,
            pltpu.SemaphoreType.REGULAR, pltpu.SemaphoreType.REGULAR,
        ],
        compiler_params=pltpu.CompilerParams(
            collective_id=0, has_side_effects=True, vmem_limit_bytes=44 * 1024 * 1024
        ),
        cost_estimate=pl.CostEstimate(
            flops=3 * 2 * 8 * block * depth * q,
            bytes_accessed=4 * depth * (q + 2 * block), transcendentals=0,
        ),
    )(*(pltpu.with_memory_space_constraint(x, pltpu.HBM) for x in (
        amplitudes, integrals, c_index.reshape(1, -1), d_index.reshape(1, -1), a_index, b_index)))
    return jnp.transpose(out, (1, 0, 2))


def solution(mesh):
    placed = (P(None, "ab", "cd"), P("cd", "ab"), P("cd"), P("cd"), P("ab"), P("ab"))
    return jax.shard_map(
        functools.partial(local, mesh.shape["cd"]), mesh=mesh, in_specs=placed,
        out_specs=P("cd", None, "ab"), check_vma=False,
    )
```
